256 devices in a mesh: dom: 64 (over y, z, core), rep: 4 (over x).
Axes of the slice: x: 4, y: 4, z: 8, core: 2. Of those that a mesh axis runs over, the one named last changes fastest.
Arguments:
- embeddings: bfloat16 [98304, 1024], P(('dom', 'rep')), may hold values from -6 to 6
- endpoint_pairs: int32 [32768, 2], P(('dom', 'rep')), may hold values from 0 to 98303, as said below
- node_slot: int32 [98304], replicated, may hold values from 0 to 98303, as said below
- first_weight: bfloat16 [2048, 1024], replicated, may hold values from -0.125 to 0.125
- second_weight: bfloat16 [1024, 1024], replicated, may hold values from -0.1875 to 0.1875
- score_weight: bfloat16 [1024], replicated, may hold values from -0.1875 to 0.1875
- score_grad: float32 [32768], P(('dom', 'rep')), may hold values from -48 to 48
Outputs:
- link_score: float32 [32768], P(('dom', 'rep'))
- node_grad: float32 [98304, 1024], P(('dom', 'rep'))
- first_grad: float32 [2048, 1024], P(('dom', 'rep'))
- second_grad: float32 [1024, 1024], P(('dom', 'rep'))
- head_grad: float32 [1024], replicated
The draws below stay inside these ranges and needn't reach their ends.
Inputs may be any that keep to these rules, and one draw needn't show every extreme that they name: node_slot is a permutation of the table positions; position s is held by the device of index s // 384 over dom+rep. `endpoint_pairs`: among the endpoints of one side of the pairs of one device, at most 2 have positions held by any one device, and in every such group some device holds exactly 2.
All inputs are finite; a program needn't handle non-finite values.
Results may differ from the reference program's by a relative error of at most 0.005.
Values may be sent and summed in bfloat16 or wider, within the bound.
A program may use at most 128 MiB of HBM per device.

```python
import jax
import jax.numpy as jnp
from jax import lax

D = 1024
H = 1024
NODE_DEV = 384
EDGE_DEV = 128
NODES = 98304
EDGES = 32768
CAP = 2


def owner_list(seed_key):
    device_total = EDGES // EDGE_DEV
    key_star, key_rest, key_mix = jax.random.split(seed_key, 3)
    star = jax.random.randint(key_star, (), 0, device_total).astype(jnp.int32)
    others = jax.random.permutation(key_rest, (device_total - 1) * CAP)[:EDGE_DEV - CAP].astype(jnp.int32) // CAP
    others = others + (others >= star).astype(jnp.int32)
    listing = jnp.concatenate([jnp.full((CAP,), star, jnp.int32), others])
    return jax.random.permutation(key_mix, listing)


def shared_layout(seed_key):
    device_total = EDGES // EDGE_DEV
    slot_key = jax.random.fold_in(seed_key, 11)
    slot_table = jax.random.permutation(slot_key, NODES).astype(jnp.int32)
    node_of_slot = jnp.argsort(slot_table).astype(jnp.int32)
    owner_key = jax.random.fold_in(seed_key, 12)
    owner_keys = jax.random.split(owner_key, device_total * 2)
    owners = jax.vmap(owner_list)(owner_keys).reshape(device_total, 2, EDGE_DEV)
    owners = jnp.transpose(owners, (0, 2, 1))
    row_key = jax.random.fold_in(seed_key, 13)
    local_rows = jax.random.randint(row_key, (device_total, EDGE_DEV, 2), 0, NODE_DEV).astype(jnp.int32)
    positions = owners * NODE_DEV + local_rows
    pairs = node_of_slot[positions].reshape(EDGES, 2)
    return (slot_table, pairs)


def draw_node_slot(key, part):
    return shared_layout(key)[0]


def draw_endpoint_pairs(key, part):
    return shared_layout(key)[1]


def block_scale(rng, extent, cuts, least, top_value):
    gain = 1.0
    for axis_at, shards_of in cuts:
        heights = jax.random.uniform(jax.random.fold_in(jax.random.fold_in(rng, 6), axis_at), (shards_of,), jnp.float32, least / len(cuts), top_value / len(cuts))
        gain = gain * jnp.repeat(jnp.exp(heights), extent[axis_at] // shards_of).reshape((-1,) + (1,) * (len(extent) - 1 - axis_at))
    return gain


def centred(stream_key, extent, width, reach, shards=(), held_as=jnp.bfloat16):
    gain = block_scale(stream_key, extent, shards, -0.22, 0.18) if shards else 1.0
    values = jax.random.normal(stream_key, extent, jnp.float32) * width * gain
    return jnp.minimum(jnp.maximum(values, -reach), reach).astype(held_as)


def setup_inputs(seed: int = 0) -> dict:
    seeds = jax.random.split(jax.random.key(seed), 8)
    return {
        "embeddings": centred(seeds[0], (NODES, D), 1.0, 6.0, ((0, 256),)),
        "endpoint_pairs": draw_endpoint_pairs(jax.random.fold_in(seeds[7], 71), 0),
        "node_slot": draw_node_slot(jax.random.fold_in(seeds[7], 71), 0),
        "first_weight": centred(seeds[3], (2 * D, H), (2 * D) ** -0.5, 0.125),
        "second_weight": centred(seeds[4], (H, H), H ** -0.5, 0.1875),
        "score_weight": centred(seeds[5], (H,), H ** -0.5, 0.1875),
        "score_grad": centred(seeds[6], (EDGES,), 8.0, 48.0, ((0, 256),), jnp.float32),
    }


def gelu_slope(values):
    return jax.jvp(jax.nn.gelu, (values,), (jnp.ones_like(values),))


def reference(embeddings, endpoint_pairs, node_slot, first_weight, second_weight, score_weight, score_grad):
    block_edges = min(EDGES, 4096)
    block_count = EDGES // block_edges
    slot_pairs = node_slot[endpoint_pairs].astype(jnp.int32).reshape(block_count, block_edges, 2)
    cot_blocks = score_grad.reshape(block_count, block_edges)
    head_f = score_weight.astype(jnp.float32)

    def one_block(carry, block):
        grad_first, grad_second, grad_head, table_grad = carry
        slot_block, cot_block = block
        features = embeddings[slot_block].reshape(block_edges, 2 * D)
        first_pre = jnp.dot(features, first_weight, preferred_element_type=jnp.float32)
        first_val, first_slope = gelu_slope(first_pre)
        first_act = first_val.astype(jnp.bfloat16)
        second_pre = jnp.dot(first_act, second_weight, preferred_element_type=jnp.float32)
        second_val, second_slope = gelu_slope(second_pre)
        second_act = second_val.astype(jnp.bfloat16)
        scores = jnp.dot(second_act, score_weight, preferred_element_type=jnp.float32)
        grad_head = grad_head + jnp.dot(cot_block, second_act.astype(jnp.float32), precision=lax.Precision.HIGHEST)
        second_delta = (cot_block[:, None] * head_f[None, :] * second_slope).astype(jnp.bfloat16)
        grad_second = grad_second + jnp.dot(first_act.T, second_delta, preferred_element_type=jnp.float32)
        first_delta = (jnp.dot(second_delta, second_weight.T, preferred_element_type=jnp.float32) * first_slope).astype(jnp.bfloat16)
        grad_first = grad_first + jnp.dot(features.T, first_delta, preferred_element_type=jnp.float32)
        feature_grad = jnp.dot(first_delta, first_weight.T, preferred_element_type=jnp.float32)
        table_grad = table_grad.at[slot_block.reshape(-1)].add(feature_grad.reshape(block_edges * 2, D))
        return (grad_first, grad_second, grad_head, table_grad), scores

    start = (jnp.zeros((2 * D, H), jnp.float32), jnp.zeros((H, H), jnp.float32),
             jnp.zeros((H,), jnp.float32), jnp.zeros((NODES, D), jnp.float32))
    final, scores = lax.scan(one_block, start, (slot_pairs, cot_blocks))
    grad_first, grad_second, grad_head, table_grad = final
    return scores.reshape(EDGES), table_grad, grad_first, grad_second, grad_head
```

```python
import functools

import jax
import jax.numpy as jnp
from jax import lax
from jax.experimental import pallas as pl
from jax.experimental.pallas import tpu as pltpu
from jax.sharding import PartitionSpec as P

MESH = pl.DeviceIdType.MESH
NY, NZ, NC, NX = 4, 8, 2, 4
NZC, NXY = NZ * NC, NX * NY
NDEV = NZC * NXY
ROWS, WIDTH, HID, EDGES = 384, 1024, 1024, 128
BF, F32 = jnp.bfloat16, jnp.float32
GELU_A, GELU_B = 0.7978845608028654, 0.044715


def dot(a, b):
    return jnp.dot(a, b, preferred_element_type=F32)


def dot_nt(a, b):
    return lax.dot_general(a, b, (((1,), (1,)), ((), ())), preferred_element_type=F32)


def dot_tn(a, b):
    return lax.dot_general(a, b, (((0,), (0,)), ((), ())), preferred_element_type=F32)


def gelu_both(v):
    t = jnp.tanh(GELU_A * (v + GELU_B * (v * v * v)))
    half = 0.5 * (1.0 + t)
    slope = half + 0.5 * v * (1.0 - t * t) * (GELU_A * (1.0 + (3.0 * GELU_B) * (v * v)))
    return v * half, slope


def iota(shape, dim):
    return lax.broadcasted_iota(jnp.int32, shape, dim)


def body(
    code_row, code_col, sgrad_col, sw_row, emb_hbm, w1_hbm, w2_hbm,
    score_out, node_out, first_out, second_out, head_out,
    emb, w1, w2, idx, hot, stage, send_g, recv_g, send_r, recv_r,
    feats, first_act, first_slope, second_act, ft_own, ft, at_own, at, d1, d2, fg,
    pa, pb, ra, rb, sa, sb, r2a, r2b, ta, tb, r3a, r3b, hbuf,
    small, load_sem, ss, rs,
):
    dom = lax.axis_index("dom")
    x = lax.axis_index("rep")
    y, z, c = dom // 16, (dom // 2) % 8, dom % 2
    zc = z * 2 + c
    xy = y * 4 + x
    me = xy * 16 + zc

    def ident(yy, zz, cc, xx):
        return ((yy * 8 + zz) * 2 + cc, xx)

    def zc_peer(k):
        return ident(y, (z + k % 8) % 8, (c + k // 8) % 2, x)

    def xy_peer(k):
        return ident((y + k // 4) % 4, z, c, (x + k % 4) % 4)

    def rcopy(src, dst, sem, dev):
        return pltpu.make_async_remote_copy(
            src_ref=src, dst_ref=dst, send_sem=ss.at[sem], recv_sem=rs.at[sem],
            device_id=dev, device_id_type=MESH,
        )

    def wait_send(ref, sem):
        pltpu.make_async_copy(ref, ref, ss.at[sem]).wait()

    def wait_recv(ref, sem):
        pltpu.make_async_copy(ref, ref, rs.at[sem]).wait()

    loads = [
        pltpu.make_async_copy(emb_hbm, emb, load_sem.at[0]),
        pltpu.make_async_copy(w1_hbm, w1, load_sem.at[1]),
        pltpu.make_async_copy(w2_hbm, w2, load_sem.at[2]),
    ]
    for load in loads:
        load.start()
    idx[pl.ds(me, 1), :] = code_row[...]
    bar = pltpu.get_barrier_semaphore()

    @pl.loop(1, 16)
    def _(k):
        pl.semaphore_signal(bar, inc=1, device_id=zc_peer(k), device_id_type=MESH)
        pl.semaphore_signal(bar, inc=1, device_id=xy_peer(k), device_id_type=MESH)

    pl.semaphore_wait(bar, 30)

    @pl.loop(1, 16)
    def _(k):
        row = idx.at[pl.ds(me, 1)]
        rcopy(row, row, 0, zc_peer(k)).start()

    wait_recv(small, 0)

    @pl.loop(1, 16)
    def _(k):
        rows = idx.at[pl.ds(xy * 16, 16)]
        rcopy(rows, rows, 1, xy_peer(k)).start()

    wait_recv(idx.at[pl.ds(0, 240)], 1)
    wait_send(small, 0)
    wait_send(idx.at[pl.ds(0, 240)], 1)

    before = (iota((128, 128), 0) < iota((128, 128), 1)).astype(BF)
    loads[0].wait()
    for side in range(2):
        codes = idx[:, side * 128:(side + 1) * 128]
        mine = (codes >> 9) == me
        rank = dot(mine.astype(BF), before)
        local = ((codes & 511) + 1).astype(F32)
        for k in range(2):
            s = side * 2 + k
            hit = mine & (rank == float(k))
            want = jnp.sum(jnp.where(hit, local, 0.0), axis=1, keepdims=True).astype(jnp.int32) - 1
            hot[s] = (want == iota((NDEV, ROWS), 1)).astype(BF)

    def spread(s, n, part):
        for h in range(2):
            stage[h, pl.ds(s * 4 + n, NDEV, stride=16), :] = part[:, h * 128:(h + 1) * 128]

    def pack(dst):
        @pl.loop(0, 16)
        def _(i):
            rows = pl.ds(i * 256, 256)
            both = jnp.concatenate([stage[0, rows, :], stage[1, rows, :]], axis=1)
            dst[pl.ds(i * 16, 16)] = both.astype(BF).reshape(16, 16, 256)

    def unpack(src):
        @pl.loop(0, 16)
        def _(i):
            rows = pl.ds(i * 256, 256)
            both = src[pl.ds(i * 16, 16)].reshape(256, 256).astype(F32)
            stage[0, rows, :] = both[:, :128]
            stage[1, rows, :] = both[:, 128:]

    def collect(s, n):
        rows = pl.ds(s * 4 + n, NDEV, stride=16)
        return jnp.concatenate([stage[0, rows, :], stage[1, rows, :]], axis=1).astype(BF)

    def exchange(src, dst, sem, keep_sem):
        own = pltpu.make_async_copy(src.at[me], dst.at[me], load_sem.at[keep_sem])
        own.start()

        @pl.loop(1, NDEV)
        def _(k):
            yy = (y + (k // 32) % 4) % 4
            xx = (x + (k // 8) % 4) % 4
            zz = (z + k % 8) % 8
            cc = (c + k // 128) % 2
            to = (yy * 4 + xx) * 16 + zz * 2 + cc
            rcopy(src.at[to], dst.at[me], sem, ident(yy, zz, cc, xx)).start()

        return own

    for s in range(4):
        for n in range(4):
            spread(s, n, dot(hot[s], emb[:, n * 256:(n + 1) * 256]))
    pack(send_g)
    own_g = exchange(send_g, recv_g, 2, 3)

    earlier = iota((128, 128), 1) < iota((128, 128), 0)
    picks = []
    for side in range(2):
        row_owner = code_row[:, side * 128:(side + 1) * 128] >> 9
        col_owner = code_col[:, side:side + 1] >> 9
        rank = jnp.sum(jnp.where((col_owner == row_owner) & earlier, 1.0, 0.0), axis=1, keepdims=True)
        home = col_owner == iota((128, NDEV), 1)
        for k in range(2):
            picks.append((home & (rank == float(k))).astype(BF))
    loads[1].wait()
    loads[2].wait()

    own_g.wait()
    wait_recv(recv_g.at[pl.ds(0, 255)], 2)
    unpack(recv_g)
    other = ident(y, z, 1 - c, x)
    for side in range(2):
        for n in range(4):
            col = side * 1024 + n * 256
            part = dot(picks[side * 2], collect(side * 2, n)) + dot(picks[side * 2 + 1], collect(side * 2 + 1, n))
            part = part.astype(BF)
            feats[:, col:col + 256] = part
            ft_own[(col // 64):(col // 64) + 4] = part.T.reshape(4, 2, 32, 128)
    rcopy(ft_own.at[:, 1 - c], ft.at[:, :, pl.ds(128, 128)], 3, other).start()
    ft[:, :, 0:128] = ft_own[:, c]

    for n in range(4):
        cols = slice(n * 256, (n + 1) * 256)
        act, slope = gelu_both(dot(feats[...], w1[:, cols]))
        act = act.astype(BF)
        first_act[:, cols] = act
        first_slope[:, cols] = slope
        at_own[n * 8:(n + 1) * 8] = act.T.reshape(8, 2, 16, 128)
    rcopy(at_own.at[:, 1 - c], at.at[:, :, pl.ds(128, 128)], 4, other).start()
    at[:, :, 0:128] = at_own[:, c]

    score = jnp.zeros((1, 128), F32)
    sgrad = sgrad_col[...]
    for n in range(4):
        cols = slice(n * 256, (n + 1) * 256)
        act, slope = gelu_both(dot(first_act[...], w2[:, cols]))
        act = act.astype(BF)
        sw = sw_row[:, cols]
        score += dot_nt(jnp.broadcast_to(sw, (8, 256)), act)[0:1]
        hbuf[0, :, cols] = jnp.sum(sgrad * act.astype(F32), axis=0, keepdims=True)
        d2[0:128, cols] = (sgrad * sw.astype(F32) * slope).astype(BF)
    score_out[...] = score
    rcopy(d2.at[pl.ds(0, 128)], d2.at[pl.ds(128, 128)], 5, other).start()
    rcopy(hbuf.at[0], hbuf.at[1], 6, other).start()

    for n in range(4):
        cols = slice(n * 256, (n + 1) * 256)
        back = dot_nt(d2[0:128, :], w2[cols, :])
        d1[0:128, cols] = (back * first_slope[:, cols]).astype(BF)
    rcopy(d1.at[pl.ds(0, 128)], d1.at[pl.ds(128, 128)], 7, other).start()

    for n in range(8):
        fg[:, n * 256:(n + 1) * 256] = dot_nt(d1[0:128, :], w1[n * 256:(n + 1) * 256, :]).astype(BF)
    for s in range(4):
        for n in range(4):
            col = (s // 2) * 1024 + n * 256
            spread(s, n, dot_tn(picks[s], fg[:, col:col + 256]))
    pack(send_r)

    wait_recv(at.at[:, :, pl.ds(0, 128)], 4)
    wait_recv(d2.at[pl.ds(0, 128)], 5)
    low = iota((8, 8, 512), 1) < 4
    for yy in range(4):
        res = dot(at[yy * 8:(yy + 1) * 8].reshape(128, 256), d2[...]).reshape(8, 16, 1024)
        for pair in range(2):
            lo = res[:, pair * 8:(pair + 1) * 8, :512]
            hi = res[:, pair * 8:(pair + 1) * 8, 512:]
            even = jnp.where(low, lo, pltpu.roll(hi, 4, axis=1))
            odd = jnp.where(low, pltpu.roll(lo, 4, axis=1), hi)
            for bit, part in ((0, even), (1, odd)):
                full = jnp.concatenate([part[:, :, :256], part[:, :, 256:]], axis=1)
                pb[yy, pair * 2 + bit, :, :, 128:384] = full.astype(BF)
    wait_recv(ft.at[:, :, pl.ds(0, 128)], 3)
    wait_recv(d1.at[pl.ds(0, 128)], 7)
    for yy in range(4):
        lhs = ft[yy * 8:(yy + 1) * 8].reshape(256, 256)
        for n in range(2):
            lo = dot(lhs, d1[:, n * 256:(n + 1) * 256]).reshape(8, 4, 8, 256)
            hi = dot(lhs, d1[:, 512 + n * 256:512 + (n + 1) * 256]).reshape(8, 4, 8, 256)
            for xx in range(4):
                full = jnp.concatenate([lo[:, xx], hi[:, xx]], axis=1).astype(BF)
                if n == 0:
                    pa[xx, yy, :, :, 0:256] = full
                else:
                    pa[xx, yy, :, :, 256:384] = full[:, :, :128]
                    pb[yy, xx, :, :, 0:128] = full[:, :, 128:]

    def along(axis, k):
        if axis == "x":
            return ident(y, z, c, (x + k) % 4), (x + k) % 4
        if axis == "y":
            return ident((y + k) % 4, z, c, x), (y + k) % 4
        return ident(y, (z + k) % 8, c, x), (z + k) % 8

    for k in range(1, 4):
        dev, at_x = along("x", k)
        rcopy(pa.at[at_x], ra.at[k - 1], 8, dev).start()
        dev, at_y = along("y", k)
        rcopy(pb.at[at_y], rb.at[k - 1], 9, dev).start()

    own_r = exchange(send_r, recv_r, 10, 4)

    def head_step(base, count, axis, mine, sem):
        for k in range(1, count):
            dev, _ = along(axis, k)
            rcopy(hbuf.at[base + mine], hbuf.at[base + mine], sem, dev).start()

    wait_recv(hbuf.at[0], 6)
    wait_send(hbuf.at[0], 6)
    hbuf[2 + x] = hbuf[0] + hbuf[1]
    head_step(2, 4, "x", x, 11)

    def add4(own, got, out, sec):
        total = own[sec].astype(F32) + got[0, sec].astype(F32) + got[1, sec].astype(F32) + got[2, sec].astype(F32)
        out[sec] = total.astype(BF)

    wait_recv(ra, 8)

    @pl.loop(0, 4)
    def _(i):
        add4(pa.at[x], ra, sa, i)

    for k in range(1, 4):
        dev, at_y = along("y", k)
        rcopy(sa.at[at_y], r2a.at[k - 1], 12, dev).start()
    wait_recv(rb, 9)

    @pl.loop(0, 4)
    def _(i):
        add4(pb.at[y], rb, sb, i)

    for k in range(1, 4):
        dev, at_x = along("x", k)
        rcopy(sb.at[at_x], r2b.at[k - 1], 13, dev).start()

    wait_recv(hbuf.at[pl.ds(2, 3)], 11)
    wait_send(hbuf.at[pl.ds(2, 3)], 11)
    hbuf[6 + y] = hbuf[2] + hbuf[3] + hbuf[4] + hbuf[5]
    head_step(6, 4, "y", y, 14)

    wait_recv(r2a, 12)
    total = sa[y].astype(F32) + r2a[0].astype(F32) + r2a[1].astype(F32) + r2a[2].astype(F32)
    ta[...] = total.astype(BF)
    for k in range(1, 8):
        dev, at_z = along("z", k)
        rcopy(ta.at[at_z], r3a.at[k - 1], 15, dev).start()
    wait_recv(r2b, 13)
    total = sb[x].astype(F32) + r2b[0].astype(F32) + r2b[1].astype(F32) + r2b[2].astype(F32)
    tb[...] = total.astype(BF)
    for k in range(1, 8):
        dev, at_z = along("z", k)
        rcopy(tb.at[at_z], r3b.at[k - 1], 16, dev).start()

    wait_recv(hbuf.at[pl.ds(6, 3)], 14)
    wait_send(hbuf.at[pl.ds(6, 3)], 14)
    hbuf[10 + z] = hbuf[6] + hbuf[7] + hbuf[8] + hbuf[9]
    head_step(10, 8, "z", z, 17)

    wait_recv(r3a, 15)
    wait_recv(r3b, 16)
    left = ta[z].astype(F32)
    right = tb[z].astype(F32)
    for k in range(7):
        left += r3a[k].astype(F32)
        right += r3b[k].astype(F32)
    whole = jnp.concatenate([left, right], axis=1)
    first_out[:, 0:512] = whole[0:8, 0:512]
    first_out[:, 512:1024] = whole[8:16, 0:512]
    second_out[:, 0:256] = whole[0:4, 512:768]
    second_out[:, 512:768] = whole[4:8, 512:768]
    second_out[:, 256:512] = whole[8:12, 512:768]
    second_out[:, 768:1024] = whole[12:16, 512:768]

    wait_recv(hbuf.at[pl.ds(10, 7)], 17)
    head = hbuf[10]
    for k in range(1, 8):
        head += hbuf[10 + k]
    head_out[...] = head

    own_r.wait()
    wait_recv(recv_r.at[pl.ds(0, 255)], 10)
    unpack(recv_r)
    for n in range(4):
        total = dot_tn(hot[0], collect(0, n))
        for s in range(1, 4):
            total += dot_tn(hot[s], collect(s, n))
        node_out[:, n * 256:(n + 1) * 256] = total

    wait_send(send_g.at[pl.ds(0, 255)], 2)
    wait_send(ft.at[:, :, pl.ds(0, 128)], 3)
    wait_send(at.at[:, :, pl.ds(0, 128)], 4)
    wait_send(d2.at[pl.ds(0, 128)], 5)
    wait_send(d1.at[pl.ds(0, 128)], 7)
    wait_send(ra, 8)
    wait_send(rb, 9)
    wait_send(send_r.at[pl.ds(0, 255)], 10)
    wait_send(r2a, 12)
    wait_send(r2b, 13)
    wait_send(r3a, 15)
    wait_send(r3b, 16)
    wait_send(hbuf.at[pl.ds(10, 7)], 17)


def shards(
    embeddings, endpoint_pairs, node_slot, first_weight, second_weight, score_weight, score_grad
):
    slots = node_slot[endpoint_pairs]
    owner = slots // ROWS
    local = slots - owner * ROWS
    oy, oz, oc, ox = owner // 64, (owner // 8) % 8, (owner // 4) % 2, owner % 4
    code = ((oy * 4 + ox) * 16 + oz * 2 + oc) * 512 + local
    vm = pl.BlockSpec(memory_space=pltpu.VMEM)
    hbm = pl.BlockSpec(memory_space=pl.ANY)
    V = pltpu.VMEM
    scratch = [
        V((ROWS, WIDTH), BF), V((2 * WIDTH, HID), BF), V((HID, HID), BF),
        V((NDEV, 2 * EDGES), jnp.int32), V((4, NDEV, ROWS), BF), V((2, NDEV * 16, 128), F32),
        V((NDEV, 16, 256), BF), V((NDEV, 16, 256), BF), V((NDEV, 16, 256), BF), V((NDEV, 16, 256), BF),
        V((EDGES, 2 * WIDTH), BF), V((EDGES, HID), BF), V((EDGES, HID), F32), V((EDGES, HID), BF),
        V((32, 2, 32, EDGES), BF), V((32, 32, 2 * EDGES), BF),
        V((32, 2, 16, EDGES), BF), V((32, 16, 2 * EDGES), BF),
        V((2 * EDGES, HID), BF), V((2 * EDGES, HID), BF), V((EDGES, 2 * WIDTH), BF),
        V((4, 4, 8, 16, 384), BF), V((4, 4, 8, 16, 384), BF),
        V((3, 4, 8, 16, 384), BF), V((3, 4, 8, 16, 384), BF),
        V((4, 8, 16, 384), BF), V((4, 8, 16, 384), BF),
        V((3, 8, 16, 384), BF), V((3, 8, 16, 384), BF),
        V((8, 16, 384), BF), V((8, 16, 384), BF),
        V((7, 16, 384), BF), V((7, 16, 384), BF),
        V((18, 1, HID), F32),
        V((15, 1, 2 * EDGES), jnp.int32),
        pltpu.SemaphoreType.DMA((5,)), pltpu.SemaphoreType.DMA((18,)), pltpu.SemaphoreType.DMA((18,)),
    ]
    score, node, first, second, head = pl.pallas_call(
        body,
        out_shape=(
            jax.ShapeDtypeStruct((1, EDGES), F32),
            jax.ShapeDtypeStruct((ROWS, WIDTH), F32),
            jax.ShapeDtypeStruct((8, HID), F32),
            jax.ShapeDtypeStruct((4, HID), F32),
            jax.ShapeDtypeStruct((1, HID), F32),
        ),
        in_specs=[vm] * 4 + [hbm] * 3,
        out_specs=(vm,) * 5,
        scratch_shapes=scratch,
        compiler_params=pltpu.CompilerParams(
            collective_id=0, has_side_effects=True, vmem_limit_bytes=56 * 2**20
        ),
    )(
        code.T.reshape(1, 2 * EDGES), code, score_grad.reshape(EDGES, 1), score_weight.reshape(1, HID),
        embeddings, first_weight, second_weight,
    )
    return score.reshape(EDGES), node, first, second, head.reshape(HID)


def solution(mesh):
    both = P(("dom", "rep"))
    rows = P(("dom", "rep"), None)
    return jax.shard_map(
        shards,
        mesh=mesh,
        in_specs=(rows, rows, P(), P(), P(), P(), both),
        out_specs=(both, rows, rows, rows, P()),
        check_vma=False,
    )
```

```python
import functools

import jax
import jax.numpy as jnp
from jax import lax
from jax.experimental import pallas as pl
from jax.experimental.pallas import tpu as pltpu
from jax.sharding import PartitionSpec as P

MESH = pl.DeviceIdType.MESH
NY, NZ, NC, NX = 4, 8, 2, 4
NZC, NXY = NZ * NC, NX * NY
NDEV = NZC * NXY
NODES = 98304
ROWS, WIDTH, HID, EDGES = 384, 1024, 1024, 128
BF, F32 = jnp.bfloat16, jnp.float32
GELU_A, GELU_B = 0.7978845608028654, 0.044715


def dot(a, b):
    return jnp.dot(a, b, preferred_element_type=F32)


def dot_nt(a, b):
    return lax.dot_general(a, b, (((1,), (1,)), ((), ())), preferred_element_type=F32)


def dot_tn(a, b):
    return lax.dot_general(a, b, (((0,), (0,)), ((), ())), preferred_element_type=F32)


def gelu_both(v):
    t = jnp.tanh(GELU_A * (v + GELU_B * (v * v * v)))
    half = 0.5 * (1.0 + t)
    slope = half + 0.5 * v * (1.0 - t * t) * (GELU_A * (1.0 + (3.0 * GELU_B) * (v * v)))
    return v * half, slope


def iota(shape, dim):
    return lax.broadcasted_iota(jnp.int32, shape, dim)


def body(
    pairs, sgrad_in, sw_in, table_hbm, emb_hbm, w1_hbm, w2_hbm,
    node_out, small_out,
    table, emb, w1, w2, w1t, w2t, idx, hot, hot_t, picks, picks_t, stage,
    send_g, recv_g, send_r, recv_r,
    feats, first_act, first_slope, ft_own, ft, at_own, at, d1, d2, fg,
    pa, pb, ra, rb, ua, ub, sa, sb, r2a, r2b, ta, tb, r3a, r3b, hbuf,
    fifteen, load_sem, ss, rs,
):
    dom = lax.axis_index("dom")
    x = lax.axis_index("rep")
    y, z, c = dom // 16, (dom // 2) % 8, dom % 2
    zc = z * 2 + c
    xy = y * 4 + x
    me = xy * 16 + zc

    def ident(yy, zz, cc, xx):
        return ((yy * 8 + zz) * 2 + cc, xx)

    def zc_peer(k):
        return ident(y, (z + k % 8) % 8, (c + k // 8) % 2, x)

    def xy_peer(k):
        return ident((y + k // 4) % 4, z, c, (x + k % 4) % 4)

    def rcopy(src, dst, sem, dev):
        return pltpu.make_async_remote_copy(
            src_ref=src, dst_ref=dst, send_sem=ss.at[sem], recv_sem=rs.at[sem],
            device_id=dev, device_id_type=MESH,
        )

    def wait_send(ref, sem):
        pltpu.make_async_copy(ref, ref, ss.at[sem]).wait()

    def wait_recv(ref, sem):
        pltpu.make_async_copy(ref, ref, rs.at[sem]).wait()

    loads = [
        pltpu.make_async_copy(table_hbm, table, load_sem.at[0]),
        pltpu.make_async_copy(emb_hbm, emb, load_sem.at[1]),
        pltpu.make_async_copy(w1_hbm, w1, load_sem.at[2]),
        pltpu.make_async_copy(w2_hbm, w2, load_sem.at[3]),
    ]
    for load in loads:
        load.start()
    bar = pltpu.get_barrier_semaphore()

    for k in range(1, 16):
        pl.semaphore_signal(bar, inc=1, device_id=zc_peer(k), device_id_type=MESH)
        pl.semaphore_signal(bar, inc=1, device_id=xy_peer(k), device_id_type=MESH)

    eye = iota((128, 128), 0) == iota((128, 128), 1)
    lanes = iota((128, 128), 1)
    loads[0].wait()
    slots = table[...]
    digits = jnp.concatenate(
        [(slots & 255).astype(F32), ((slots >> 8) & 255).astype(F32), (slots >> 16).astype(F32)], axis=1
    ).astype(BF)
    col_code, row_code = [], []
    for side in range(2):
        node_id = pairs[side:side + 1, :].astype(F32)
        node_id = jnp.sum(jnp.where(eye, node_id, 0.0), axis=1, keepdims=True).astype(jnp.int32)
        rows = ((node_id >> 7) == iota((128, NODES // 128), 1)).astype(F32).astype(BF)
        got = dot(rows, digits)
        slot = got[:, 0:128] + 256.0 * got[:, 128:256] + 65536.0 * got[:, 256:384]
        slot = jnp.sum(jnp.where(lanes == (node_id & 127), slot, 0.0), axis=1, keepdims=True)
        owner = ((slot + 0.5) * (1.0 / ROWS)).astype(jnp.int32)
        local = slot.astype(jnp.int32) - owner * ROWS
        quick = ((owner >> 6) * 4 + (owner & 3)) * 16 + ((owner >> 2) & 15)
        code = quick * 512 + local
        row = jnp.sum(jnp.where(eye, code.astype(F32), 0.0), axis=0, keepdims=True).astype(jnp.int32)
        col_code.append(code)
        row_code.append(row)

    idx[pl.ds(me, 1), :] = jnp.concatenate(row_code, axis=1)
    pl.semaphore_wait(bar, 30)

    for k in range(1, 16):
        row = idx.at[pl.ds(me, 1)]
        rcopy(row, row, 0, zc_peer(k)).start()

    wait_recv(fifteen, 0)

    for k in range(1, 16):
        rows = idx.at[pl.ds(xy * 16, 16)]
        rcopy(rows, rows, 1, xy_peer(k)).start()

    wait_recv(idx.at[pl.ds(0, 240)], 1)

    before = (iota((128, 128), 0) < iota((128, 128), 1)).astype(F32).astype(BF)
    for side in range(2):
        codes = idx[:, side * 128:(side + 1) * 128]
        mine = (codes >> 9) == me
        rank = dot(mine.astype(F32).astype(BF), before)
        local = ((codes & 511) + 1).astype(F32)
        for k in range(2):
            s = side * 2 + k
            hit = mine & (rank == float(k))
            found = jnp.sum(jnp.where(hit, local, 0.0), axis=1, keepdims=True).astype(jnp.int32) - 1
            for b in range(4):
                hot[b, s * 64:(s + 1) * 64, :] = (
                    (found[b * 64:(b + 1) * 64] == iota((64, ROWS), 1)).astype(F32).astype(BF)
                )

    def spread(s, n, part):
        for h in range(2):
            stage[h, pl.ds(s * 4 + n, 64, stride=16), :] = part[:, h * 128:(h + 1) * 128]

    def pack(dst, b):
        @pl.loop(0, 4)
        def _(i):
            rows = pl.ds(i * 256, 256)
            both = jnp.concatenate([stage[0, rows, :], stage[1, rows, :]], axis=1)
            dst[pl.ds(b * 64 + i * 16, 16)] = both.astype(BF).reshape(16, 16, 256)

    def unpack(src, b):
        @pl.loop(0, 4)
        def _(i):
            rows = pl.ds(i * 256, 256)
            both = src[pl.ds(b * 64 + i * 16, 16)].reshape(256, 256).astype(F32)
            stage[0, rows, :] = both[:, :128]
            stage[1, rows, :] = both[:, 128:]

    def collect(ss, n):
        out = []
        for s in ss:
            rows = pl.ds(s * 4 + n, 64, stride=16)
            out.append(jnp.concatenate([stage[0, rows, :], stage[1, rows, :]], axis=1))
        return jnp.concatenate(out, axis=0).astype(BF)

    def send_block(src, dst, j, sem):
        yy = (y + j) % 4

        @pl.loop(0, 8)
        def _(k):
            xx = (x + k % 4) % 4
            cc = (c + k // 4) % 2

            def push(zz):
                to = (yy * 4 + xx) * 16 + zz * 2 + cc
                rcopy(src.at[to], dst.at[me], sem + j, ident(yy, zz, cc, xx)).start()

            @pl.when(j + k > 0)
            def _():
                push(z)

            for i in range(1, 8):
                push((z + i) % 8)

    def wait_block(dst, j, sem):
        @pl.when(j == 0)
        def _():
            wait_recv(dst.at[pl.ds(0, 63)], sem)

        @pl.when(j > 0)
        def _():
            wait_recv(dst.at[pl.ds(0, 64)], sem + j)

    def wait_block_sent(src, sem):
        wait_send(src.at[pl.ds(0, 63)], sem)
        for j in range(1, 4):
            wait_send(src.at[pl.ds(0, 64)], sem + j)

    G, R = 2, 6
    loads[1].wait()

    @pl.loop(0, 4)
    def _(j):
        b = (y + j) % 4
        for n in range(4):
            part = dot(hot[b], emb[:, n * 256:(n + 1) * 256])
            for s in range(4):
                spread(s, n, part[s * 64:(s + 1) * 64])
        pack(send_g, b)
        send_block(send_g, recv_g, j, G)

    recv_g[me] = send_g[me]

    earlier = iota((128, 128), 1) < iota((128, 128), 0)
    for side in range(2):
        row_owner = row_code[side] >> 9
        col_owner = col_code[side] >> 9
        rank = jnp.sum(jnp.where((col_owner == row_owner) & earlier, 1.0, 0.0), axis=1, keepdims=True)
        for b in range(4):
            home = col_owner == b * 64 + (lanes & 63)
            pick = jnp.where(home & (rank == (lanes >> 6).astype(F32)), 1.0, 0.0)
            picks[b, side] = pick.astype(BF)
            picks_t[b, side] = pick.T.astype(BF)
    feats[...] = jnp.zeros_like(feats)

    @pl.loop(0, 4)
    def _(b):
        hot_t[b] = hot[b].T

    loads[2].wait()
    loads[3].wait()

    @pl.loop(0, 8)
    def _(i):
        rows = pl.ds(pl.multiple_of(i * 256, 256), 256)
        for n in range(4):
            w1t[n * 256:(n + 1) * 256, rows] = w1[rows, n * 256:(n + 1) * 256].T

    @pl.loop(0, 4)
    def _(i):
        rows = pl.ds(pl.multiple_of(i * 256, 256), 256)
        for n in range(4):
            w2t[n * 256:(n + 1) * 256, rows] = w2[rows, n * 256:(n + 1) * 256].T

    @pl.loop(0, 4)
    def _(j):
        b = (y + 4 - j) % 4
        wait_block(recv_g, j, G)
        unpack(recv_g, b)
        for side in range(2):
            for n in range(4):
                cols = slice(side * 1024 + n * 256, side * 1024 + (n + 1) * 256)
                part = dot(picks[b, side], collect((side * 2, side * 2 + 1), n))
                feats[:, cols] = feats[:, cols] + part.astype(BF)

    other = ident(y, z, 1 - c, x)
    for n in range(4):
        cols = slice(n * 256, (n + 1) * 256)
        act, slope = gelu_both(dot(feats[...], w1[:, cols]))
        act = act.astype(BF)
        first_act[:, cols] = act
        first_slope[:, cols] = slope

    score = jnp.zeros((1, 128), F32)
    sgrad = jnp.sum(jnp.where(eye, sgrad_in[...], 0.0), axis=1, keepdims=True)
    for n in range(4):
        cols = slice(n * 256, (n + 1) * 256)
        act, slope = gelu_both(dot(first_act[...], w2[:, cols]))
        act = act.astype(BF)
        sw = sw_in[cols].reshape(1, 256)
        score += dot_nt(jnp.broadcast_to(sw, (8, 256)), act)[0:1]
        hbuf[0, :, cols] = jnp.sum(sgrad * act.astype(F32), axis=0, keepdims=True)
        d2[0:128, cols] = (sgrad * sw.astype(F32) * slope).astype(BF)
    small_out[13:14, 0:128] = score
    rcopy(d2.at[pl.ds(0, 128)], d2.at[pl.ds(128, 128)], 12, other).start()
    rcopy(hbuf.at[0], hbuf.at[1], 13, other).start()

    for n in range(4):
        cols = slice(n * 256, (n + 1) * 256)
        back = dot(d2[0:128, :], w2t[:, cols])
        d1[0:128, cols] = (back * first_slope[:, cols]).astype(BF)
    rcopy(d1.at[pl.ds(0, 128)], d1.at[pl.ds(128, 128)], 14, other).start()

    for n in range(8):
        cols = slice(n * 256, (n + 1) * 256)
        fg[:, cols] = dot(d1[0:128, :], w1t[:, cols]).astype(BF)

    def return_block(j):
        b = (y + j) % 4
        for side in range(2):
            for n in range(4):
                col = side * 1024 + n * 256
                part = dot(picks_t[b, side], fg[:, col:col + 256])
                for k in range(2):
                    spread(side * 2 + k, n, part[k * 64:(k + 1) * 64])
        pack(send_r, b)
        send_block(send_r, recv_r, j, R)

    @pl.loop(0, 1)
    def _(j):
        return_block(j)

    for i in range(4):
        cols = slice(i * 256, (i + 1) * 256)
        at_own[i * 8:(i + 1) * 8] = first_act[:, cols].T.reshape(8, 2, 16, 128)
    rcopy(at_own.at[:, 1 - c], at.at[:, :, pl.ds(128, 128)], 11, other).start()
    at[:, :, 0:128] = at_own[:, c]
    for i in range(8):
        cols = slice(i * 256, (i + 1) * 256)
        ft_own[i * 4:(i + 1) * 4] = feats[:, cols].T.reshape(4, 2, 32, 128)
    rcopy(ft_own.at[:, 1 - c], ft.at[:, :, pl.ds(128, 128)], 10, other).start()
    ft[:, :, 0:128] = ft_own[:, c]

    wait_recv(at.at[:, :, pl.ds(0, 128)], 11)
    wait_recv(d2.at[pl.ds(0, 128)], 12)
    low = iota((8, 8, 512), 1) < 4

    @pl.loop(0, 4)
    def _(yy):
        res = dot(at[pl.ds(yy * 8, 8)].reshape(128, 256), d2[...]).reshape(8, 16, 1024)
        for pair in range(2):
            lo = res[:, pair * 8:(pair + 1) * 8, :512]
            hi = res[:, pair * 8:(pair + 1) * 8, 512:]
            even = jnp.where(low, lo, pltpu.roll(hi, 4, axis=1))
            odd = jnp.where(low, pltpu.roll(lo, 4, axis=1), hi)
            for bit, part in ((0, even), (1, odd)):
                full = jnp.concatenate([part[:, :, :256], part[:, :, 256:]], axis=1)
                pb[yy, pair * 2 + bit, :, :, 128:384] = full.astype(BF)

    wait_recv(ft.at[:, :, pl.ds(0, 128)], 10)
    wait_recv(d1.at[pl.ds(0, 128)], 14)

    @pl.loop(0, 4)
    def _(yy):
        lhs = ft[pl.ds(yy * 8, 8)].reshape(256, 256)
        for n in range(2):
            lo = dot(lhs, d1[:, n * 256:(n + 1) * 256]).reshape(8, 4, 8, 256)
            hi = dot(lhs, d1[:, 512 + n * 256:512 + (n + 1) * 256]).reshape(8, 4, 8, 256)
            for xx in range(4):
                full = jnp.concatenate([lo[:, xx], hi[:, xx]], axis=1).astype(BF)
                if n == 0:
                    pa[xx, yy, :, :, 0:256] = full
                else:
                    pa[xx, yy, :, :, 256:384] = full[:, :, :128]
                    pb[yy, xx, :, :, 0:128] = full[:, :, 128:]

    def along(axis, k):
        if axis == "x":
            return ident(y, z, c, (x + k) % 4), (x + k) % 4
        if axis == "y":
            return ident((y + k) % 4, z, c, x), (y + k) % 4
        return ident(y, (z + k) % 8, c, x), (z + k) % 8

    near, far = pl.ds(0, 2), pl.ds(2, 2)
    for axis, mine, buf, got, aug, sem in (("x", x, pa, ra, ua, 15), ("y", y, pb, rb, ub, 16)):
        right, to_right = along(axis, 1)
        left, to_left = along(axis, 3)
        opposite = (mine + 2) % 4
        rcopy(buf.at[opposite, near], aug.at[0], sem + 9, right).start()
        rcopy(buf.at[opposite, far], aug.at[1], sem + 9, left).start()
        rcopy(buf.at[to_right, far], got.at[0, far], sem, right).start()
        rcopy(buf.at[to_left, near], got.at[1, near], sem, left).start()
    @pl.loop(1, 2)
    def _(j):
        return_block(j)

    for axis, mine, buf, got, aug, sem in (("x", x, pa, ra, ua, 15), ("y", y, pb, rb, ub, 16)):
        right, to_right = along(axis, 1)
        left, to_left = along(axis, 3)
        wait_recv(aug, sem + 9)

        @pl.loop(0, 2)
        def _(i):
            buf[to_right, i] = (buf[to_right, i].astype(F32) + aug[0, i].astype(F32)).astype(BF)
            buf[to_left, 2 + i] = (buf[to_left, 2 + i].astype(F32) + aug[1, i].astype(F32)).astype(BF)

        rcopy(buf.at[to_right, near], got.at[0, near], sem, right).start()
        rcopy(buf.at[to_left, far], got.at[1, far], sem, left).start()

    @pl.loop(2, 4)
    def _(j):
        return_block(j)

    recv_r[me] = send_r[me]

    def head_step(base, count, axis, mine, sem):
        for k in range(1, count):
            dev, _ = along(axis, k)
            rcopy(hbuf.at[base + mine], hbuf.at[base + mine], sem, dev).start()

    wait_recv(hbuf.at[0], 13)
    wait_send(hbuf.at[0], 13)
    hbuf[2 + x] = hbuf[0] + hbuf[1]
    head_step(2, 4, "x", x, 17)

    def add3(own, got, out, sec):
        total = own[sec].astype(F32) + got[0, sec].astype(F32) + got[1, sec].astype(F32)
        out[sec] = total.astype(BF)

    node_out[...] = jnp.zeros_like(node_out)

    def land_block(j):
        b = (y + 4 - j) % 4
        wait_block(recv_r, j, R)
        unpack(recv_r, b)
        for n in range(4):
            cols = slice(n * 256, (n + 1) * 256)
            node_out[:, cols] = node_out[:, cols] + dot(hot_t[b], collect((0, 1, 2, 3), n))

    wait_recv(ra, 15)

    @pl.loop(0, 4)
    def _(i):
        add3(pa.at[x], ra, sa, i)

    for k in range(1, 4):
        dev, at_y = along("y", k)
        rcopy(sa.at[at_y], r2a.at[k - 1], 18, dev).start()
    wait_recv(rb, 16)

    @pl.loop(0, 4)
    def _(i):
        add3(pb.at[y], rb, sb, i)

    for k in range(1, 4):
        dev, at_x = along("x", k)
        rcopy(sb.at[at_x], r2b.at[k - 1], 19, dev).start()

    @pl.loop(0, 1)
    def _(j):
        land_block(j)

    wait_recv(hbuf.at[pl.ds(2, 3)], 17)
    wait_send(hbuf.at[pl.ds(2, 3)], 17)
    hbuf[6 + y] = hbuf[2] + hbuf[3] + hbuf[4] + hbuf[5]
    head_step(6, 4, "y", y, 20)

    wait_recv(r2a, 18)
    total = sa[y].astype(F32) + r2a[0].astype(F32) + r2a[1].astype(F32) + r2a[2].astype(F32)
    ta[...] = total.astype(BF)
    for k in range(1, 8):
        dev, at_z = along("z", k)
        rcopy(ta.at[at_z], r3a.at[k - 1], 21, dev).start()
    wait_recv(r2b, 19)
    total = sb[x].astype(F32) + r2b[0].astype(F32) + r2b[1].astype(F32) + r2b[2].astype(F32)
    tb[...] = total.astype(BF)
    for k in range(1, 8):
        dev, at_z = along("z", k)
        rcopy(tb.at[at_z], r3b.at[k - 1], 22, dev).start()

    wait_recv(hbuf.at[pl.ds(6, 3)], 20)
    wait_send(hbuf.at[pl.ds(6, 3)], 20)
    hbuf[10 + z] = hbuf[6] + hbuf[7] + hbuf[8] + hbuf[9]
    head_step(10, 8, "z", z, 23)

    @pl.loop(1, 3)
    def _(j):
        land_block(j)

    wait_recv(r3a, 21)
    wait_recv(r3b, 22)
    left = ta[z].astype(F32)
    right = tb[z].astype(F32)
    for k in range(7):
        left += r3a[k].astype(F32)
        right += r3b[k].astype(F32)
    whole = jnp.concatenate([left, right], axis=1)
    small_out[0:8, 0:512] = whole[0:8, 0:512]
    small_out[0:8, 512:1024] = whole[8:16, 0:512]
    small_out[8:12, 0:256] = whole[0:4, 512:768]
    small_out[8:12, 512:768] = whole[4:8, 512:768]
    small_out[8:12, 256:512] = whole[8:12, 512:768]
    small_out[8:12, 768:1024] = whole[12:16, 512:768]

    wait_recv(hbuf.at[pl.ds(10, 7)], 23)
    head = hbuf[10]
    for k in range(1, 8):
        head += hbuf[10 + k]
    small_out[12:13, :] = head

    @pl.loop(3, 4)
    def _(j):
        land_block(j)

    wait_send(fifteen, 0)
    wait_send(idx.at[pl.ds(0, 240)], 1)
    wait_block_sent(send_g, G)
    wait_block_sent(send_r, R)
    wait_send(ft.at[:, :, pl.ds(0, 128)], 10)
    wait_send(at.at[:, :, pl.ds(0, 128)], 11)
    wait_send(d2.at[pl.ds(0, 128)], 12)
    wait_send(d1.at[pl.ds(0, 128)], 14)
    wait_send(ra, 15)
    wait_send(rb, 16)
    wait_send(ua, 24)
    wait_send(ub, 25)
    wait_send(r2a, 18)
    wait_send(r2b, 19)
    wait_send(r3a, 21)
    wait_send(r3b, 22)
    wait_send(hbuf.at[pl.ds(10, 7)], 23)


def deliver(node_in, small_in, score_out, node_out, first_out, second_out, head_out, held, small, sem_in, sem_out):
    spans = [pl.ds(i * 96, 96) for i in range(4)]
    ins = [pltpu.make_async_copy(node_in.at[p], held.at[p], sem_in.at[i]) for i, p in enumerate(spans)]
    outs = [pltpu.make_async_copy(held.at[p], node_out.at[p], sem_out.at[i]) for i, p in enumerate(spans)]
    rest = pltpu.make_async_copy(small_in, small, sem_in.at[4])
    for copy in ins + [rest]:
        copy.start()
    for i in range(4):
        ins[i].wait()
        outs[i].start()
    rest.wait()
    score_out[...] = small[13:14, 0:128].reshape(128)
    first_out[...] = small[0:8, :]
    second_out[...] = small[8:12, :]
    head_out[...] = small[12:13, :].reshape(HID)
    for copy in outs:
        copy.wait()


def shards(
    embeddings, endpoint_pairs, node_slot, first_weight, second_weight, score_weight, score_grad
):
    vm = pl.BlockSpec(memory_space=pltpu.VMEM)
    hbm = pl.BlockSpec(memory_space=pltpu.HBM)
    V = pltpu.VMEM
    scratch = [
        V((NODES // 128, 128), jnp.int32), V((ROWS, WIDTH), BF), V((2 * WIDTH, HID), BF), V((HID, HID), BF),
        V((HID, 2 * WIDTH), BF), V((HID, HID), BF),
        V((NDEV, 2 * EDGES), jnp.int32), V((4, NDEV, ROWS), BF), V((4, ROWS, NDEV), BF),
        V((4, 2, EDGES, 128), BF), V((4, 2, 128, EDGES), BF), V((2, 64 * 16, 128), F32),
        V((NDEV, 16, 256), BF), V((NDEV, 16, 256), BF), V((NDEV, 16, 256), BF), V((NDEV, 16, 256), BF),
        V((EDGES, 2 * WIDTH), BF), V((EDGES, HID), BF), V((EDGES, HID), F32),
        V((32, 2, 32, EDGES), BF), V((32, 32, 2 * EDGES), BF),
        V((32, 2, 16, EDGES), BF), V((32, 16, 2 * EDGES), BF),
        V((2 * EDGES, HID), BF), V((2 * EDGES, HID), BF), V((EDGES, 2 * WIDTH), BF),
        V((4, 4, 8, 16, 384), BF), V((4, 4, 8, 16, 384), BF),
        V((2, 4, 8, 16, 384), BF), V((2, 4, 8, 16, 384), BF),
        V((2, 2, 8, 16, 384), BF), V((2, 2, 8, 16, 384), BF),
        V((4, 8, 16, 384), BF), V((4, 8, 16, 384), BF),
        V((3, 8, 16, 384), BF), V((3, 8, 16, 384), BF),
        V((8, 16, 384), BF), V((8, 16, 384), BF),
        V((7, 16, 384), BF), V((7, 16, 384), BF),
        V((18, 1, HID), F32),
        V((15, 1, 2 * EDGES), jnp.int32),
        pltpu.SemaphoreType.DMA((4,)), pltpu.SemaphoreType.DMA((26,)), pltpu.SemaphoreType.DMA((26,)),
    ]
    node, small = pl.pallas_call(
        body,
        out_shape=(
            jax.ShapeDtypeStruct((ROWS, WIDTH), F32),
            jax.ShapeDtypeStruct((16, HID), F32),
        ),
        in_specs=[vm] * 3 + [hbm] * 4,
        out_specs=(vm, vm),
        scratch_shapes=scratch,
        compiler_params=pltpu.CompilerParams(
            collective_id=0, has_side_effects=True, vmem_limit_bytes=58 * 2**20
        ),
    )(
        endpoint_pairs.T, score_grad.reshape(1, EDGES), score_weight,
        node_slot.reshape(NODES // 128, 128), embeddings, first_weight, second_weight,
    )
    return pl.pallas_call(
        deliver,
        out_shape=(
            jax.ShapeDtypeStruct((EDGES,), F32),
            jax.ShapeDtypeStruct((ROWS, WIDTH), F32),
            jax.ShapeDtypeStruct((8, HID), F32),
            jax.ShapeDtypeStruct((4, HID), F32),
            jax.ShapeDtypeStruct((HID,), F32),
        ),
        in_specs=[hbm, hbm],
        out_specs=(vm, hbm, vm, vm, vm),
        scratch_shapes=[
            V((ROWS, WIDTH), F32), V((16, HID), F32), pltpu.SemaphoreType.DMA((5,)), pltpu.SemaphoreType.DMA((4,)),
        ],
    )(node, small)


def solution(mesh):
    both = P(("dom", "rep"))
    rows = P(("dom", "rep"), None)
    return jax.shard_map(
        shards,
        mesh=mesh,
        in_specs=(rows, rows, P(), P(), P(), P(), both),
        out_specs=(both, rows, rows, rows, P()),
        check_vma=False,
    )
```

```python
import functools

import jax
import jax.numpy as jnp
from jax import lax
from jax.experimental import pallas as pl
from jax.experimental.pallas import tpu as pltpu
from jax.sharding import PartitionSpec as P

MESH = pl.DeviceIdType.MESH
NY, NZ, NC, NX = 4, 8, 2, 4
NZC, NXY = NZ * NC, NX * NY
NDEV = NZC * NXY
NODES = 98304
ROWS, WIDTH, HID, EDGES = 384, 1024, 1024, 128
BF, F32 = jnp.bfloat16, jnp.float32
GELU_A, GELU_B = 0.7978845608028654, 0.044715


def dot(a, b):
    return jnp.dot(a, b, preferred_element_type=F32)


def dot_nt(a, b):
    return lax.dot_general(a, b, (((1,), (1,)), ((), ())), preferred_element_type=F32)


def dot_tn(a, b):
    return lax.dot_general(a, b, (((0,), (0,)), ((), ())), preferred_element_type=F32)


def gelu_both(v):
    t = jnp.tanh(GELU_A * (v + GELU_B * (v * v * v)))
    half = 0.5 * (1.0 + t)
    slope = half + 0.5 * v * (1.0 - t * t) * (GELU_A * (1.0 + (3.0 * GELU_B) * (v * v)))
    return v * half, slope


def iota(shape, dim):
    return lax.broadcasted_iota(jnp.int32, shape, dim)


def body(
    pairs, sgrad_in, sw_in, table_hbm, emb_hbm, w1_hbm, w2_hbm,
    node_out, small_out,
    table, emb, w1, w2, w1t, w2t, idx, hot, hot_t, picks, picks_t, stage,
    send_g, recv_g, send_r, recv_r,
    feats, first_act, first_slope, ft_own, ft, at_own, at, d1, d2, fg,
    pa, pb, ra, rb, ua, ub, sa, sb, r2a, r2b, ta, tb, r3a, r3b, hbuf,
    fifteen, load_sem, ss, rs,
):
    dom = lax.axis_index("dom")
    x = lax.axis_index("rep")
    y, z, c = dom // 16, (dom // 2) % 8, dom % 2
    zc = z * 2 + c
    xy = y * 4 + x
    me = xy * 16 + zc

    def ident(yy, zz, cc, xx):
        return ((yy * 8 + zz) * 2 + cc, xx)

    def zc_peer(k):
        return ident(y, (z + k % 8) % 8, (c + k // 8) % 2, x)

    def xy_peer(k):
        return ident((y + k // 4) % 4, z, c, (x + k % 4) % 4)

    def rcopy(src, dst, sem, dev):
        return pltpu.make_async_remote_copy(
            src_ref=src, dst_ref=dst, send_sem=ss.at[sem], recv_sem=rs.at[sem],
            device_id=dev, device_id_type=MESH,
        )

    def wait_send(ref, sem):
        pltpu.make_async_copy(ref, ref, ss.at[sem]).wait()

    def wait_recv(ref, sem):
        pltpu.make_async_copy(ref, ref, rs.at[sem]).wait()

    loads = [
        pltpu.make_async_copy(table_hbm, table, load_sem.at[0]),
        pltpu.make_async_copy(emb_hbm, emb, load_sem.at[1]),
        pltpu.make_async_copy(w1_hbm, w1, load_sem.at[2]),
        pltpu.make_async_copy(w2_hbm, w2, load_sem.at[3]),
    ]
    loads[0].start()
    bar = pltpu.get_barrier_semaphore()

    for k in range(1, 16):
        pl.semaphore_signal(bar, inc=1, device_id=zc_peer(k), device_id_type=MESH)
        pl.semaphore_signal(bar, inc=1, device_id=xy_peer(k), device_id_type=MESH)

    eye = iota((128, 128), 0) == iota((128, 128), 1)
    lanes = iota((128, 128), 1)
    loads[0].wait()
    for load in loads[1:]:
        load.start()
    slots = table[...]
    digits = jnp.concatenate(
        [(slots & 255).astype(F32), ((slots >> 8) & 255).astype(F32), (slots >> 16).astype(F32)], axis=1
    ).astype(BF)
    col_code, row_code = [], []
    for side in range(2):
        node_id = pairs[side:side + 1, :].astype(F32)
        node_id = jnp.sum(jnp.where(eye, node_id, 0.0), axis=1, keepdims=True).astype(jnp.int32)
        rows = ((node_id >> 7) == iota((128, NODES // 128), 1)).astype(F32).astype(BF)
        got = dot(rows, digits)
        slot = got[:, 0:128] + 256.0 * got[:, 128:256] + 65536.0 * got[:, 256:384]
        slot = jnp.sum(jnp.where(lanes == (node_id & 127), slot, 0.0), axis=1, keepdims=True)
        owner = ((slot + 0.5) * (1.0 / ROWS)).astype(jnp.int32)
        local = slot.astype(jnp.int32) - owner * ROWS
        quick = ((owner >> 6) * 4 + (owner & 3)) * 16 + ((owner >> 2) & 15)
        code = quick * 512 + local
        row = jnp.sum(jnp.where(eye, code.astype(F32), 0.0), axis=0, keepdims=True).astype(jnp.int32)
        col_code.append(code)
        row_code.append(row)

    idx[pl.ds(me, 1), :] = jnp.concatenate(row_code, axis=1)
    pl.semaphore_wait(bar, 30)

    for k in range(1, 16):
        row = idx.at[pl.ds(me, 1)]
        rcopy(row, row, 0, zc_peer(k)).start()

    wait_recv(fifteen, 0)

    for k in range(1, 16):
        rows = idx.at[pl.ds(xy * 16, 16)]
        rcopy(rows, rows, 1, xy_peer(k)).start()

    wait_recv(idx.at[pl.ds(0, 240)], 1)

    before = (iota((128, 128), 0) < iota((128, 128), 1)).astype(F32).astype(BF)
    for side in range(2):
        codes = idx[:, side * 128:(side + 1) * 128]
        mine = (codes >> 9) == me
        rank = dot(mine.astype(F32).astype(BF), before)
        local = ((codes & 511) + 1).astype(F32)
        for k in range(2):
            s = side * 2 + k
            hit = mine & (rank == float(k))
            found = jnp.sum(jnp.where(hit, local, 0.0), axis=1, keepdims=True).astype(jnp.int32) - 1
            for b in range(4):
                hot[b, s * 64:(s + 1) * 64, :] = (
                    (found[b * 64:(b + 1) * 64] == iota((64, ROWS), 1)).astype(F32).astype(BF)
                )

    def spread(s, n, part):
        for h in range(2):
            stage[h, pl.ds(s * 4 + n, 64, stride=16), :] = part[:, h * 128:(h + 1) * 128]

    def pack(dst, b):
        @pl.loop(0, 4)
        def _(i):
            rows = pl.ds(i * 256, 256)
            both = jnp.concatenate([stage[0, rows, :], stage[1, rows, :]], axis=1)
            dst[pl.ds(b * 64 + i * 16, 16)] = both.astype(BF).reshape(16, 16, 256)

    def unpack(src, b):
        @pl.loop(0, 4)
        def _(i):
            rows = pl.ds(i * 256, 256)
            both = src[pl.ds(b * 64 + i * 16, 16)].reshape(256, 256).astype(F32)
            stage[0, rows, :] = both[:, :128]
            stage[1, rows, :] = both[:, 128:]

    def collect(ss, n):
        out = []
        for s in ss:
            rows = pl.ds(s * 4 + n, 64, stride=16)
            out.append(jnp.concatenate([stage[0, rows, :], stage[1, rows, :]], axis=1))
        return jnp.concatenate(out, axis=0).astype(BF)

    def send_block(src, dst, j, sem, first=0, last=8):
        yy = (y + j) % 4

        @pl.loop(first, last)
        def _(k):
            xx = (x + k % 4) % 4
            cc = (c + k // 4) % 2

            def push(zz):
                to = (yy * 4 + xx) * 16 + zz * 2 + cc
                rcopy(src.at[to], dst.at[me], sem + j, ident(yy, zz, cc, xx)).start()

            @pl.when(j + k > 0)
            def _():
                push(z)

            for i in range(1, 8):
                push((z + i) % 8)

    def wait_block(dst, j, sem):
        @pl.when(j == 0)
        def _():
            wait_recv(dst.at[pl.ds(0, 63)], sem)

        @pl.when(j > 0)
        def _():
            wait_recv(dst.at[pl.ds(0, 64)], sem + j)

    def wait_block_sent(src, sem):
        wait_send(src.at[pl.ds(0, 63)], sem)
        for j in range(1, 4):
            wait_send(src.at[pl.ds(0, 64)], sem + j)

    G, R = 2, 6
    loads[1].wait()

    @pl.loop(0, 4)
    def _(j):
        b = (y + j) % 4
        for n in range(4):
            part = dot(hot[b], emb[:, n * 256:(n + 1) * 256])
            for s in range(4):
                spread(s, n, part[s * 64:(s + 1) * 64])
        pack(send_g, b)
        send_block(send_g, recv_g, j, G)

    recv_g[me] = send_g[me]

    earlier = iota((128, 128), 1) < iota((128, 128), 0)
    for side in range(2):
        row_owner = row_code[side] >> 9
        col_owner = col_code[side] >> 9
        rank = jnp.sum(jnp.where((col_owner == row_owner) & earlier, 1.0, 0.0), axis=1, keepdims=True)
        for b in range(4):
            home = col_owner == b * 64 + (lanes & 63)
            pick = jnp.where(home & (rank == (lanes >> 6).astype(F32)), 1.0, 0.0)
            picks[b, side] = pick.astype(BF)
            picks_t[b, side] = pick.T.astype(BF)
    feats[...] = jnp.zeros_like(feats)

    @pl.loop(0, 4)
    def _(b):
        hot_t[b] = hot[b].T

    loads[2].wait()
    loads[3].wait()

    @pl.loop(0, 8)
    def _(i):
        rows = pl.ds(pl.multiple_of(i * 256, 256), 256)
        for n in range(4):
            w1t[n * 256:(n + 1) * 256, rows] = w1[rows, n * 256:(n + 1) * 256].T

    @pl.loop(0, 4)
    def _(i):
        rows = pl.ds(pl.multiple_of(i * 256, 256), 256)
        for n in range(4):
            w2t[n * 256:(n + 1) * 256, rows] = w2[rows, n * 256:(n + 1) * 256].T

    @pl.loop(0, 4)
    def _(j):
        b = (y + 4 - j) % 4
        wait_block(recv_g, j, G)
        unpack(recv_g, b)
        for side in range(2):
            for n in range(4):
                cols = slice(side * 1024 + n * 256, side * 1024 + (n + 1) * 256)
                part = dot(picks[b, side], collect((side * 2, side * 2 + 1), n))
                feats[:, cols] = feats[:, cols] + part.astype(BF)

    other = ident(y, z, 1 - c, x)
    for n in range(4):
        cols = slice(n * 256, (n + 1) * 256)
        act, slope = gelu_both(dot(feats[...], w1[:, cols]))
        act = act.astype(BF)
        first_act[:, cols] = act
        first_slope[:, cols] = slope

    score = jnp.zeros((1, 128), F32)
    sgrad = jnp.sum(jnp.where(eye, sgrad_in[...], 0.0), axis=1, keepdims=True)
    for n in range(4):
        cols = slice(n * 256, (n + 1) * 256)
        act, slope = gelu_both(dot(first_act[...], w2[:, cols]))
        act = act.astype(BF)
        sw = sw_in[cols].reshape(1, 256)
        score += dot_nt(jnp.broadcast_to(sw, (8, 256)), act)[0:1]
        hbuf[0, :, cols] = jnp.sum(sgrad * act.astype(F32), axis=0, keepdims=True)
        d2[0:128, cols] = (sgrad * sw.astype(F32) * slope).astype(BF)
    small_out[13:14, 0:128] = score
    rcopy(d2.at[pl.ds(0, 128)], d2.at[pl.ds(128, 128)], 12, other).start()
    rcopy(hbuf.at[0], hbuf.at[1], 13, other).start()

    for n in range(4):
        cols = slice(n * 256, (n + 1) * 256)
        back = dot(d2[0:128, :], w2t[:, cols])
        d1[0:128, cols] = (back * first_slope[:, cols]).astype(BF)
    rcopy(d1.at[pl.ds(0, 128)], d1.at[pl.ds(128, 128)], 14, other).start()

    for n in range(8):
        cols = slice(n * 256, (n + 1) * 256)
        fg[:, cols] = dot(d1[0:128, :], w1t[:, cols]).astype(BF)

    def return_pack(j):
        b = (y + j) % 4
        for side in range(2):
            for n in range(4):
                col = side * 1024 + n * 256
                part = dot(picks_t[b, side], fg[:, col:col + 256])
                for k in range(2):
                    spread(side * 2 + k, n, part[k * 64:(k + 1) * 64])
        pack(send_r, b)

    def groups(first, last):
        for i in range(first, last):
            if i % 4 == 0:
                return_pack(i // 4)
            send_block(send_r, recv_r, i // 4, R, i % 4 * 2, i % 4 * 2 + 2)

    groups(0, 2)

    for i in range(4):
        cols = slice(i * 256, (i + 1) * 256)
        at_own[i * 8:(i + 1) * 8] = first_act[:, cols].T.reshape(8, 2, 16, 128)
    rcopy(at_own.at[:, 1 - c], at.at[:, :, pl.ds(128, 128)], 11, other).start()
    at[:, :, 0:128] = at_own[:, c]
    for i in range(8):
        cols = slice(i * 256, (i + 1) * 256)
        ft_own[i * 4:(i + 1) * 4] = feats[:, cols].T.reshape(4, 2, 32, 128)
    rcopy(ft_own.at[:, 1 - c], ft.at[:, :, pl.ds(128, 128)], 10, other).start()
    ft[:, :, 0:128] = ft_own[:, c]

    wait_recv(at.at[:, :, pl.ds(0, 128)], 11)
    wait_recv(d2.at[pl.ds(0, 128)], 12)
    low = iota((8, 8, 512), 1) < 4

    @pl.loop(0, 4)
    def _(yy):
        res = dot(at[pl.ds(yy * 8, 8)].reshape(128, 256), d2[...]).reshape(8, 16, 1024)
        for pair in range(2):
            lo = res[:, pair * 8:(pair + 1) * 8, :512]
            hi = res[:, pair * 8:(pair + 1) * 8, 512:]
            even = jnp.where(low, lo, pltpu.roll(hi, 4, axis=1))
            odd = jnp.where(low, pltpu.roll(lo, 4, axis=1), hi)
            for bit, part in ((0, even), (1, odd)):
                full = jnp.concatenate([part[:, :, :256], part[:, :, 256:]], axis=1)
                pb[yy, pair * 2 + bit, :, :, 128:384] = full.astype(BF)

    wait_recv(ft.at[:, :, pl.ds(0, 128)], 10)
    wait_recv(d1.at[pl.ds(0, 128)], 14)

    @pl.loop(0, 4)
    def _(yy):
        lhs = ft[pl.ds(yy * 8, 8)].reshape(256, 256)
        for n in range(2):
            lo = dot(lhs, d1[:, n * 256:(n + 1) * 256]).reshape(8, 4, 8, 256)
            hi = dot(lhs, d1[:, 512 + n * 256:512 + (n + 1) * 256]).reshape(8, 4, 8, 256)
            for xx in range(4):
                full = jnp.concatenate([lo[:, xx], hi[:, xx]], axis=1).astype(BF)
                if n == 0:
                    pa[xx, yy, :, :, 0:256] = full
                else:
                    pa[xx, yy, :, :, 256:384] = full[:, :, :128]
                    pb[yy, xx, :, :, 0:128] = full[:, :, 128:]

    def along(axis, k):
        if axis == "x":
            return ident(y, z, c, (x + k) % 4), (x + k) % 4
        if axis == "y":
            return ident((y + k) % 4, z, c, x), (y + k) % 4
        return ident(y, (z + k) % 8, c, x), (z + k) % 8

    near, far = pl.ds(0, 2), pl.ds(2, 2)
    stages = (("x", x, pa, ra, ua, 15), ("y", y, pb, rb, ub, 16))
    for axis, mine, buf, got, aug, sem in stages:
        right, to_right = along(axis, 1)
        left, to_left = along(axis, 3)
        opposite = (mine + 2) % 4
        rcopy(buf.at[opposite, near], aug.at[0], sem + 9, right).start()
        rcopy(buf.at[opposite, far], aug.at[1], sem + 9, left).start()
        rcopy(buf.at[to_right, far], got.at[0, far], sem, right).start()
        rcopy(buf.at[to_left, near], got.at[1, near], sem, left).start()

    def head_step(base, count, axis, mine, sem):
        for k in range(1, count):
            dev, _ = along(axis, k)
            rcopy(hbuf.at[base + mine], hbuf.at[base + mine], sem, dev).start()

    wait_recv(hbuf.at[0], 13)
    wait_send(hbuf.at[0], 13)
    hbuf[2 + x] = hbuf[0] + hbuf[1]
    head_step(2, 4, "x", x, 17)

    groups(2, 6)

    for axis, mine, buf, got, aug, sem in stages:
        right, to_right = along(axis, 1)
        left, to_left = along(axis, 3)
        wait_recv(aug, sem + 9)

        @pl.loop(0, 2)
        def _(i):
            buf[to_right, i] = (buf[to_right, i].astype(F32) + aug[0, i].astype(F32)).astype(BF)
            buf[to_left, 2 + i] = (buf[to_left, 2 + i].astype(F32) + aug[1, i].astype(F32)).astype(BF)

        rcopy(buf.at[to_right, near], got.at[0, near], sem, right).start()
        rcopy(buf.at[to_left, far], got.at[1, far], sem, left).start()

    wait_recv(hbuf.at[pl.ds(2, 3)], 17)
    wait_send(hbuf.at[pl.ds(2, 3)], 17)
    hbuf[6 + y] = hbuf[2] + hbuf[3] + hbuf[4] + hbuf[5]
    head_step(6, 4, "y", y, 20)

    groups(6, 9)

    node_out[...] = jnp.zeros_like(node_out)

    def land_block(j):
        b = (y + 4 - j) % 4
        wait_block(recv_r, j, R)
        unpack(recv_r, b)
        for n in range(4):
            cols = slice(n * 256, (n + 1) * 256)
            node_out[:, cols] = node_out[:, cols] + dot(hot_t[b], collect((0, 1, 2, 3), n))

    def add3(own, got, out, sec):
        total = own[sec].astype(F32) + got[0, sec].astype(F32) + got[1, sec].astype(F32)
        out[sec] = total.astype(BF)

    wait_recv(ra, 15)

    @pl.loop(0, 4)
    def _(i):
        add3(pa.at[x], ra, sa, i)

    for k in range(1, 4):
        dev, at_y = along("y", k)
        rcopy(sa.at[at_y], r2a.at[k - 1], 18, dev).start()
    wait_recv(rb, 16)

    @pl.loop(0, 4)
    def _(i):
        add3(pb.at[y], rb, sb, i)

    for k in range(1, 4):
        dev, at_x = along("x", k)
        rcopy(sb.at[at_x], r2b.at[k - 1], 19, dev).start()

    groups(9, 12)

    wait_recv(hbuf.at[pl.ds(6, 3)], 20)
    wait_send(hbuf.at[pl.ds(6, 3)], 20)
    hbuf[10 + z] = hbuf[6] + hbuf[7] + hbuf[8] + hbuf[9]
    head_step(10, 8, "z", z, 23)

    wait_recv(r2a, 18)
    total = sa[y].astype(F32) + r2a[0].astype(F32) + r2a[1].astype(F32) + r2a[2].astype(F32)
    ta[...] = total.astype(BF)
    for k in range(1, 8):
        dev, at_z = along("z", k)
        rcopy(ta.at[at_z], r3a.at[k - 1], 21, dev).start()
    wait_recv(r2b, 19)
    total = sb[x].astype(F32) + r2b[0].astype(F32) + r2b[1].astype(F32) + r2b[2].astype(F32)
    tb[...] = total.astype(BF)
    for k in range(1, 8):
        dev, at_z = along("z", k)
        rcopy(tb.at[at_z], r3b.at[k - 1], 22, dev).start()

    groups(12, 16)
    recv_r[me] = send_r[me]

    @pl.loop(0, 3)
    def _(j):
        land_block(j)

    wait_recv(r3a, 21)
    wait_recv(r3b, 22)
    left = ta[z].astype(F32)
    right = tb[z].astype(F32)
    for k in range(7):
        left += r3a[k].astype(F32)
        right += r3b[k].astype(F32)
    whole = jnp.concatenate([left, right], axis=1)
    small_out[0:8, 0:512] = whole[0:8, 0:512]
    small_out[0:8, 512:1024] = whole[8:16, 0:512]
    small_out[8:12, 0:256] = whole[0:4, 512:768]
    small_out[8:12, 512:768] = whole[4:8, 512:768]
    small_out[8:12, 256:512] = whole[8:12, 512:768]
    small_out[8:12, 768:1024] = whole[12:16, 512:768]

    wait_recv(hbuf.at[pl.ds(10, 7)], 23)
    head = hbuf[10]
    for k in range(1, 8):
        head += hbuf[10 + k]
    small_out[12:13, :] = head

    @pl.loop(3, 4)
    def _(j):
        land_block(j)

    wait_send(fifteen, 0)
    wait_send(idx.at[pl.ds(0, 240)], 1)
    wait_block_sent(send_g, G)
    wait_block_sent(send_r, R)
    wait_send(ft.at[:, :, pl.ds(0, 128)], 10)
    wait_send(at.at[:, :, pl.ds(0, 128)], 11)
    wait_send(d2.at[pl.ds(0, 128)], 12)
    wait_send(d1.at[pl.ds(0, 128)], 14)
    wait_send(ra, 15)
    wait_send(rb, 16)
    wait_send(ua, 24)
    wait_send(ub, 25)
    wait_send(r2a, 18)
    wait_send(r2b, 19)
    wait_send(r3a, 21)
    wait_send(r3b, 22)
    wait_send(hbuf.at[pl.ds(10, 7)], 23)


def deliver(node_in, small_in, score_out, node_out, first_out, second_out, head_out, held, small, sem_in, sem_out):
    spans = [pl.ds(i * 96, 96) for i in range(4)]
    ins = [pltpu.make_async_copy(node_in.at[p], held.at[p], sem_in.at[i]) for i, p in enumerate(spans)]
    outs = [pltpu.make_async_copy(held.at[p], node_out.at[p], sem_out.at[i]) for i, p in enumerate(spans)]
    rest = pltpu.make_async_copy(small_in, small, sem_in.at[4])
    for copy in ins + [rest]:
        copy.start()
    for i in range(4):
        ins[i].wait()
        outs[i].start()
    rest.wait()
    score_out[...] = small[13:14, 0:128].reshape(128)
    first_out[...] = small[0:8, :]
    second_out[...] = small[8:12, :]
    head_out[...] = small[12:13, :].reshape(HID)
    for copy in outs:
        copy.wait()


def shards(
    embeddings, endpoint_pairs, node_slot, first_weight, second_weight, score_weight, score_grad
):
    vm = pl.BlockSpec(memory_space=pltpu.VMEM)
    hbm = pl.BlockSpec(memory_space=pltpu.HBM)
    V = pltpu.VMEM
    scratch = [
        V((NODES // 128, 128), jnp.int32), V((ROWS, WIDTH), BF), V((2 * WIDTH, HID), BF), V((HID, HID), BF),
        V((HID, 2 * WIDTH), BF), V((HID, HID), BF),
        V((NDEV, 2 * EDGES), jnp.int32), V((4, NDEV, ROWS), BF), V((4, ROWS, NDEV), BF),
        V((4, 2, EDGES, 128), BF), V((4, 2, 128, EDGES), BF), V((2, 64 * 16, 128), F32),
        V((NDEV, 16, 256), BF), V((NDEV, 16, 256), BF), V((NDEV, 16, 256), BF), V((NDEV, 16, 256), BF),
        V((EDGES, 2 * WIDTH), BF), V((EDGES, HID), BF), V((EDGES, HID), F32),
        V((32, 2, 32, EDGES), BF), V((32, 32, 2 * EDGES), BF),
        V((32, 2, 16, EDGES), BF), V((32, 16, 2 * EDGES), BF),
        V((2 * EDGES, HID), BF), V((2 * EDGES, HID), BF), V((EDGES, 2 * WIDTH), BF),
        V((4, 4, 8, 16, 384), BF), V((4, 4, 8, 16, 384), BF),
        V((2, 4, 8, 16, 384), BF), V((2, 4, 8, 16, 384), BF),
        V((2, 2, 8, 16, 384), BF), V((2, 2, 8, 16, 384), BF),
        V((4, 8, 16, 384), BF), V((4, 8, 16, 384), BF),
        V((3, 8, 16, 384), BF), V((3, 8, 16, 384), BF),
        V((8, 16, 384), BF), V((8, 16, 384), BF),
        V((7, 16, 384), BF), V((7, 16, 384), BF),
        V((18, 1, HID), F32),
        V((15, 1, 2 * EDGES), jnp.int32),
        pltpu.SemaphoreType.DMA((4,)), pltpu.SemaphoreType.DMA((26,)), pltpu.SemaphoreType.DMA((26,)),
    ]
    node, small = pl.pallas_call(
        body,
        out_shape=(
            jax.ShapeDtypeStruct((ROWS, WIDTH), F32),
            jax.ShapeDtypeStruct((16, HID), F32),
        ),
        in_specs=[vm] * 3 + [hbm] * 4,
        out_specs=(vm, vm),
        scratch_shapes=scratch,
        compiler_params=pltpu.CompilerParams(
            collective_id=0, has_side_effects=True, vmem_limit_bytes=58 * 2**20
        ),
    )(
        endpoint_pairs.T, score_grad.reshape(1, EDGES), score_weight,
        node_slot.reshape(NODES // 128, 128), embeddings, first_weight, second_weight,
    )
    return pl.pallas_call(
        deliver,
        out_shape=(
            jax.ShapeDtypeStruct((EDGES,), F32),
            jax.ShapeDtypeStruct((ROWS, WIDTH), F32),
            jax.ShapeDtypeStruct((8, HID), F32),
            jax.ShapeDtypeStruct((4, HID), F32),
            jax.ShapeDtypeStruct((HID,), F32),
        ),
        in_specs=[hbm, hbm],
        out_specs=(vm, hbm, vm, vm, vm),
        scratch_shapes=[
            V((ROWS, WIDTH), F32), V((16, HID), F32), pltpu.SemaphoreType.DMA((5,)), pltpu.SemaphoreType.DMA((4,)),
        ],
    )(node, small)


def solution(mesh):
    both = P(("dom", "rep"))
    rows = P(("dom", "rep"), None)
    return jax.shard_map(
        shards,
        mesh=mesh,
        in_specs=(rows, rows, P(), P(), P(), P(), both),
        out_specs=(both, rows, rows, rows, P()),
        check_vma=False,
    )
```

```python
import functools

import jax
import jax.numpy as jnp
from jax import lax
from jax.experimental import pallas as pl
from jax.experimental.pallas import tpu as pltpu
from jax.sharding import PartitionSpec as P

MESH = pl.DeviceIdType.MESH
NY, NZ, NC, NX = 4, 8, 2, 4
NZC, NXY = NZ * NC, NX * NY
NDEV = NZC * NXY
NODES = 98304
ROWS, WIDTH, HID, EDGES = 384, 1024, 1024, 128
BF, F32 = jnp.bfloat16, jnp.float32
GELU_A, GELU_B = 0.7978845608028654, 0.044715


def dot(a, b):
    return jnp.dot(a, b, preferred_element_type=F32)


def dot_nt(a, b):
    return lax.dot_general(a, b, (((1,), (1,)), ((), ())), preferred_element_type=F32)


def dot_tn(a, b):
    return lax.dot_general(a, b, (((0,), (0,)), ((), ())), preferred_element_type=F32)


def gelu_both(v):
    t = jnp.tanh(GELU_A * (v + GELU_B * (v * v * v)))
    half = 0.5 * (1.0 + t)
    slope = half + 0.5 * v * (1.0 - t * t) * (GELU_A * (1.0 + (3.0 * GELU_B) * (v * v)))
    return v * half, slope


def iota(shape, dim):
    return lax.broadcasted_iota(jnp.int32, shape, dim)


def body(
    pairs, sgrad_in, sw_in, table_hbm, emb_hbm, w1_hbm, w2_hbm,
    node_out, small_out,
    table, emb, w1, w2, w1t, w2t, idx, hot, hot_t, picks, picks_t, stage,
    send_g, recv_g, send_r, recv_r,
    feats, first_act, first_slope, ft_own, ft, at_own, at, d1, d2, fg,
    pa, pb, ra, rb, ua, ub, sa, sb, r2a, r2b, ta, tb, r3a, r3b, hbuf,
    fifteen, load_sem, ss, rs,
):
    dom = lax.axis_index("dom")
    x = lax.axis_index("rep")
    y, z, c = dom // 16, (dom // 2) % 8, dom % 2
    zc = z * 2 + c
    xy = y * 4 + x
    me = xy * 16 + zc

    def ident(yy, zz, cc, xx):
        return ((yy * 8 + zz) * 2 + cc, xx)

    def zc_peer(k):
        return ident(y, (z + k % 8) % 8, (c + k // 8) % 2, x)

    def xy_peer(k):
        return ident((y + k // 4) % 4, z, c, (x + k % 4) % 4)

    def rcopy(src, dst, sem, dev):
        return pltpu.make_async_remote_copy(
            src_ref=src, dst_ref=dst, send_sem=ss.at[sem], recv_sem=rs.at[sem],
            device_id=dev, device_id_type=MESH,
        )

    def wait_send(ref, sem):
        pltpu.make_async_copy(ref, ref, ss.at[sem]).wait()

    def wait_recv(ref, sem):
        pltpu.make_async_copy(ref, ref, rs.at[sem]).wait()

    loads = [
        pltpu.make_async_copy(table_hbm, table, load_sem.at[0]),
        pltpu.make_async_copy(emb_hbm, emb, load_sem.at[1]),
        pltpu.make_async_copy(w1_hbm, w1, load_sem.at[2]),
        pltpu.make_async_copy(w2_hbm, w2, load_sem.at[3]),
    ]
    loads[0].start()
    bar = pltpu.get_barrier_semaphore()

    for k in range(1, 16):
        pl.semaphore_signal(bar, inc=1, device_id=zc_peer(k), device_id_type=MESH)
        pl.semaphore_signal(bar, inc=1, device_id=xy_peer(k), device_id_type=MESH)

    eye = iota((128, 128), 0) == iota((128, 128), 1)
    lanes = iota((128, 128), 1)
    loads[0].wait()
    for load in loads[1:]:
        load.start()
    slots = table[...]
    digits = jnp.concatenate(
        [(slots & 255).astype(F32), ((slots >> 8) & 255).astype(F32), (slots >> 16).astype(F32)], axis=1
    ).astype(BF)
    col_code, row_code = [], []
    for side in range(2):
        node_id = pairs[side:side + 1, :].astype(F32)
        node_id = jnp.sum(jnp.where(eye, node_id, 0.0), axis=1, keepdims=True).astype(jnp.int32)
        rows = ((node_id >> 7) == iota((128, NODES // 128), 1)).astype(F32).astype(BF)
        got = dot(rows, digits)
        slot = got[:, 0:128] + 256.0 * got[:, 128:256] + 65536.0 * got[:, 256:384]
        slot = jnp.sum(jnp.where(lanes == (node_id & 127), slot, 0.0), axis=1, keepdims=True)
        owner = ((slot + 0.5) * (1.0 / ROWS)).astype(jnp.int32)
        local = slot.astype(jnp.int32) - owner * ROWS
        quick = ((owner >> 6) * 4 + (owner & 3)) * 16 + ((owner >> 2) & 15)
        code = quick * 512 + local
        row = jnp.sum(jnp.where(eye, code.astype(F32), 0.0), axis=0, keepdims=True).astype(jnp.int32)
        col_code.append(code)
        row_code.append(row)

    idx[pl.ds(me, 1), :] = jnp.concatenate(row_code, axis=1)
    pl.semaphore_wait(bar, 30)

    for k in range(1, 16):
        row = idx.at[pl.ds(me, 1)]
        rcopy(row, row, 0, zc_peer(k)).start()

    wait_recv(fifteen, 0)

    for k in range(1, 16):
        rows = idx.at[pl.ds(xy * 16, 16)]
        rcopy(rows, rows, 1, xy_peer(k)).start()

    wait_recv(idx.at[pl.ds(0, 240)], 1)

    before = (iota((128, 128), 0) < iota((128, 128), 1)).astype(F32).astype(BF)
    for side in range(2):
        codes = idx[:, side * 128:(side + 1) * 128]
        mine = (codes >> 9) == me
        rank = dot(mine.astype(F32).astype(BF), before)
        local = ((codes & 511) + 1).astype(F32)
        for k in range(2):
            s = side * 2 + k
            hit = mine & (rank == float(k))
            found = jnp.sum(jnp.where(hit, local, 0.0), axis=1, keepdims=True).astype(jnp.int32) - 1
            for b in range(4):
                hot[b, s * 64:(s + 1) * 64, :] = (
                    (found[b * 64:(b + 1) * 64] == iota((64, ROWS), 1)).astype(F32).astype(BF)
                )

    def spread(s, n, part):
        for h in range(2):
            stage[h, pl.ds(s * 4 + n, 64, stride=16), :] = part[:, h * 128:(h + 1) * 128]

    def pack(dst, b):
        @pl.loop(0, 4)
        def _(i):
            rows = pl.ds(i * 256, 256)
            both = jnp.concatenate([stage[0, rows, :], stage[1, rows, :]], axis=1)
            dst[pl.ds(b * 64 + i * 16, 16)] = both.astype(BF).reshape(16, 16, 256)

    def unpack(src, b):
        @pl.loop(0, 4)
        def _(i):
            rows = pl.ds(i * 256, 256)
            both = src[pl.ds(b * 64 + i * 16, 16)].reshape(256, 256).astype(F32)
            stage[0, rows, :] = both[:, :128]
            stage[1, rows, :] = both[:, 128:]

    def collect(ss, n):
        out = []
        for s in ss:
            rows = pl.ds(s * 4 + n, 64, stride=16)
            out.append(jnp.concatenate([stage[0, rows, :], stage[1, rows, :]], axis=1))
        return jnp.concatenate(out, axis=0).astype(BF)

    def send_block(src, dst, j, sem, first=0, last=8):
        yy = (y + j) % 4

        @pl.loop(first, last)
        def _(k):
            xx = (x + k % 4) % 4
            cc = (c + k // 4) % 2

            def push(zz):
                to = (yy * 4 + xx) * 16 + zz * 2 + cc
                rcopy(src.at[to], dst.at[me], sem + j, ident(yy, zz, cc, xx)).start()

            @pl.when(j + k > 0)
            def _():
                push(z)

            for i in range(1, 8):
                push((z + i) % 8)

    def wait_block(dst, j, sem):
        @pl.when(j == 0)
        def _():
            wait_recv(dst.at[pl.ds(0, 63)], sem)

        @pl.when(j > 0)
        def _():
            wait_recv(dst.at[pl.ds(0, 64)], sem + j)

    def wait_block_sent(src, sem):
        wait_send(src.at[pl.ds(0, 63)], sem)
        for j in range(1, 4):
            wait_send(src.at[pl.ds(0, 64)], sem + j)

    G, R = 2, 6
    loads[1].wait()

    @pl.loop(0, 4)
    def _(j):
        b = (y + j) % 4
        for n in range(4):
            part = dot(hot[b], emb[:, n * 256:(n + 1) * 256])
            for s in range(4):
                spread(s, n, part[s * 64:(s + 1) * 64])
        pack(send_g, b)
        send_block(send_g, recv_g, j, G)

    recv_g[me] = send_g[me]

    earlier = iota((128, 128), 1) < iota((128, 128), 0)
    for side in range(2):
        row_owner = row_code[side] >> 9
        col_owner = col_code[side] >> 9
        rank = jnp.sum(jnp.where((col_owner == row_owner) & earlier, 1.0, 0.0), axis=1, keepdims=True)
        for b in range(4):
            home = col_owner == b * 64 + (lanes & 63)
            pick = jnp.where(home & (rank == (lanes >> 6).astype(F32)), 1.0, 0.0)
            picks[b, side] = pick.astype(BF)
            picks_t[b, side] = pick.T.astype(BF)
    feats[...] = jnp.zeros_like(feats)

    @pl.loop(0, 4)
    def _(b):
        hot_t[b] = hot[b].T

    loads[2].wait()
    loads[3].wait()

    @pl.loop(0, 8)
    def _(i):
        rows = pl.ds(pl.multiple_of(i * 256, 256), 256)
        for n in range(4):
            w1t[n * 256:(n + 1) * 256, rows] = w1[rows, n * 256:(n + 1) * 256].T

    @pl.loop(0, 4)
    def _(i):
        rows = pl.ds(pl.multiple_of(i * 256, 256), 256)
        for n in range(4):
            w2t[n * 256:(n + 1) * 256, rows] = w2[rows, n * 256:(n + 1) * 256].T

    @pl.loop(0, 4)
    def _(j):
        b = (y + 4 - j) % 4
        wait_block(recv_g, j, G)
        unpack(recv_g, b)
        for side in range(2):
            for n in range(4):
                cols = slice(side * 1024 + n * 256, side * 1024 + (n + 1) * 256)
                part = dot(picks[b, side], collect((side * 2, side * 2 + 1), n))
                feats[:, cols] = feats[:, cols] + part.astype(BF)

    other = ident(y, z, 1 - c, x)
    for n in range(4):
        cols = slice(n * 256, (n + 1) * 256)
        act, slope = gelu_both(dot(feats[...], w1[:, cols]))
        act = act.astype(BF)
        first_act[:, cols] = act
        first_slope[:, cols] = slope

    score = jnp.zeros((1, 128), F32)
    sgrad = jnp.sum(jnp.where(eye, sgrad_in[...], 0.0), axis=1, keepdims=True)
    for n in range(4):
        cols = slice(n * 256, (n + 1) * 256)
        act, slope = gelu_both(dot(first_act[...], w2[:, cols]))
        act = act.astype(BF)
        sw = sw_in[cols].reshape(1, 256)
        score += dot_nt(jnp.broadcast_to(sw, (8, 256)), act)[0:1]
        hbuf[0, :, cols] = jnp.sum(sgrad * act.astype(F32), axis=0, keepdims=True)
        d2[0:128, cols] = (sgrad * sw.astype(F32) * slope).astype(BF)
    small_out[13:14, 0:128] = score
    rcopy(d2.at[pl.ds(0, 128)], d2.at[pl.ds(128, 128)], 12, other).start()
    rcopy(hbuf.at[0], hbuf.at[1], 13, other).start()

    for n in range(4):
        cols = slice(n * 256, (n + 1) * 256)
        back = dot(d2[0:128, :], w2t[:, cols])
        d1[0:128, cols] = (back * first_slope[:, cols]).astype(BF)
    rcopy(d1.at[pl.ds(0, 128)], d1.at[pl.ds(128, 128)], 14, other).start()

    for n in range(8):
        cols = slice(n * 256, (n + 1) * 256)
        fg[:, cols] = dot(d1[0:128, :], w1t[:, cols]).astype(BF)

    def return_pack(j):
        b = (y + j) % 4
        for side in range(2):
            for n in range(4):
                col = side * 1024 + n * 256
                part = dot(picks_t[b, side], fg[:, col:col + 256])
                for k in range(2):
                    spread(side * 2 + k, n, part[k * 64:(k + 1) * 64])
        pack(send_r, b)

    def groups(first, last):
        for i in range(first, last):
            if i % 4 == 0:
                return_pack(i // 4)
            send_block(send_r, recv_r, i // 4, R, i % 4 * 2, i % 4 * 2 + 2)

    groups(0, 4)

    for i in range(4):
        cols = slice(i * 256, (i + 1) * 256)
        at_own[i * 8:(i + 1) * 8] = first_act[:, cols].T.reshape(8, 2, 16, 128)
    rcopy(at_own.at[:, 1 - c], at.at[:, :, pl.ds(128, 128)], 11, other).start()
    at[:, :, 0:128] = at_own[:, c]
    for i in range(8):
        cols = slice(i * 256, (i + 1) * 256)
        ft_own[i * 4:(i + 1) * 4] = feats[:, cols].T.reshape(4, 2, 32, 128)
    rcopy(ft_own.at[:, 1 - c], ft.at[:, :, pl.ds(128, 128)], 10, other).start()
    ft[:, :, 0:128] = ft_own[:, c]

    wait_recv(at.at[:, :, pl.ds(0, 128)], 11)
    wait_recv(d2.at[pl.ds(0, 128)], 12)
    low = iota((8, 8, 512), 1) < 4

    @pl.loop(0, 4)
    def _(yy):
        res = dot(at[pl.ds(yy * 8, 8)].reshape(128, 256), d2[...]).reshape(8, 16, 1024)
        for pair in range(2):
            lo = res[:, pair * 8:(pair + 1) * 8, :512]
            hi = res[:, pair * 8:(pair + 1) * 8, 512:]
            even = jnp.where(low, lo, pltpu.roll(hi, 4, axis=1))
            odd = jnp.where(low, pltpu.roll(lo, 4, axis=1), hi)
            for bit, part in ((0, even), (1, odd)):
                full = jnp.concatenate([part[:, :, :256], part[:, :, 256:]], axis=1)
                pb[yy, pair * 2 + bit, :, :, 128:384] = full.astype(BF)

    wait_recv(ft.at[:, :, pl.ds(0, 128)], 10)
    wait_recv(d1.at[pl.ds(0, 128)], 14)

    @pl.loop(0, 4)
    def _(yy):
        lhs = ft[pl.ds(yy * 8, 8)].reshape(256, 256)
        for n in range(2):
            lo = dot(lhs, d1[:, n * 256:(n + 1) * 256]).reshape(8, 4, 8, 256)
            hi = dot(lhs, d1[:, 512 + n * 256:512 + (n + 1) * 256]).reshape(8, 4, 8, 256)
            for xx in range(4):
                full = jnp.concatenate([lo[:, xx], hi[:, xx]], axis=1).astype(BF)
                if n == 0:
                    pa[xx, yy, :, :, 0:256] = full
                else:
                    pa[xx, yy, :, :, 256:384] = full[:, :, :128]
                    pb[yy, xx, :, :, 0:128] = full[:, :, 128:]

    def along(axis, k):
        if axis == "x":
            return ident(y, z, c, (x + k) % 4), (x + k) % 4
        if axis == "y":
            return ident((y + k) % 4, z, c, x), (y + k) % 4
        return ident(y, (z + k) % 8, c, x), (z + k) % 8

    near, far = pl.ds(0, 2), pl.ds(2, 2)
    stages = (("x", x, pa, ra, ua, 15), ("y", y, pb, rb, ub, 16))
    for axis, mine, buf, got, aug, sem in stages:
        right, to_right = along(axis, 1)
        left, to_left = along(axis, 3)
        opposite = (mine + 2) % 4
        rcopy(buf.at[opposite, near], aug.at[0], sem + 9, right).start()
        rcopy(buf.at[opposite, far], aug.at[1], sem + 9, left).start()
        rcopy(buf.at[to_right, far], got.at[0, far], sem, right).start()
        rcopy(buf.at[to_left, near], got.at[1, near], sem, left).start()

    def head_step(base, count, axis, mine, sem):
        for k in range(1, count):
            dev, _ = along(axis, k)
            rcopy(hbuf.at[base + mine], hbuf.at[base + mine], sem, dev).start()

    wait_recv(hbuf.at[0], 13)
    wait_send(hbuf.at[0], 13)
    hbuf[2 + x] = hbuf[0] + hbuf[1]
    head_step(2, 4, "x", x, 17)

    groups(4, 8)

    for axis, mine, buf, got, aug, sem in stages:
        right, to_right = along(axis, 1)
        left, to_left = along(axis, 3)
        wait_recv(aug, sem + 9)

        @pl.loop(0, 2)
        def _(i):
            buf[to_right, i] = (buf[to_right, i].astype(F32) + aug[0, i].astype(F32)).astype(BF)
            buf[to_left, 2 + i] = (buf[to_left, 2 + i].astype(F32) + aug[1, i].astype(F32)).astype(BF)

        rcopy(buf.at[to_right, near], got.at[0, near], sem, right).start()
        rcopy(buf.at[to_left, far], got.at[1, far], sem, left).start()

    wait_recv(hbuf.at[pl.ds(2, 3)], 17)
    wait_send(hbuf.at[pl.ds(2, 3)], 17)
    hbuf[6 + y] = hbuf[2] + hbuf[3] + hbuf[4] + hbuf[5]
    head_step(6, 4, "y", y, 20)

    groups(8, 12)

    node_out[...] = jnp.zeros_like(node_out)

    def land_block(j):
        b = (y + 4 - j) % 4
        wait_block(recv_r, j, R)
        unpack(recv_r, b)
        for n in range(4):
            cols = slice(n * 256, (n + 1) * 256)
            node_out[:, cols] = node_out[:, cols] + dot(hot_t[b], collect((0, 1, 2, 3), n))

    def add3(own, got, out, sec):
        total = own[sec].astype(F32) + got[0, sec].astype(F32) + got[1, sec].astype(F32)
        out[sec] = total.astype(BF)

    wait_recv(ra, 15)

    @pl.loop(0, 4)
    def _(i):
        add3(pa.at[x], ra, sa, i)

    for k in range(1, 4):
        dev, at_y = along("y", k)
        rcopy(sa.at[at_y], r2a.at[k - 1], 18, dev).start()
    wait_recv(rb, 16)

    @pl.loop(0, 4)
    def _(i):
        add3(pb.at[y], rb, sb, i)

    for k in range(1, 4):
        dev, at_x = along("x", k)
        rcopy(sb.at[at_x], r2b.at[k - 1], 19, dev).start()

    groups(12, 16)
    recv_r[me] = send_r[me]

    wait_recv(hbuf.at[pl.ds(6, 3)], 20)
    wait_send(hbuf.at[pl.ds(6, 3)], 20)
    hbuf[10 + z] = hbuf[6] + hbuf[7] + hbuf[8] + hbuf[9]
    head_step(10, 8, "z", z, 23)

    @pl.loop(0, 1)
    def _(j):
        land_block(j)

    wait_recv(r2a, 18)
    total = sa[y].astype(F32) + r2a[0].astype(F32) + r2a[1].astype(F32) + r2a[2].astype(F32)
    ta[...] = total.astype(BF)
    for k in range(1, 8):
        dev, at_z = along("z", k)
        rcopy(ta.at[at_z], r3a.at[k - 1], 21, dev).start()
    wait_recv(r2b, 19)
    total = sb[x].astype(F32) + r2b[0].astype(F32) + r2b[1].astype(F32) + r2b[2].astype(F32)
    tb[...] = total.astype(BF)
    for k in range(1, 8):
        dev, at_z = along("z", k)
        rcopy(tb.at[at_z], r3b.at[k - 1], 22, dev).start()

    @pl.loop(1, 3)
    def _(j):
        land_block(j)

    wait_recv(r3a, 21)
    wait_recv(r3b, 22)
    left = ta[z].astype(F32)
    right = tb[z].astype(F32)
    for k in range(7):
        left += r3a[k].astype(F32)
        right += r3b[k].astype(F32)
    whole = jnp.concatenate([left, right], axis=1)
    small_out[0:8, 0:512] = whole[0:8, 0:512]
    small_out[0:8, 512:1024] = whole[8:16, 0:512]
    small_out[8:12, 0:256] = whole[0:4, 512:768]
    small_out[8:12, 512:768] = whole[4:8, 512:768]
    small_out[8:12, 256:512] = whole[8:12, 512:768]
    small_out[8:12, 768:1024] = whole[12:16, 512:768]

    wait_recv(hbuf.at[pl.ds(10, 7)], 23)
    head = hbuf[10]
    for k in range(1, 8):
        head += hbuf[10 + k]
    small_out[12:13, :] = head

    @pl.loop(3, 4)
    def _(j):
        land_block(j)

    wait_send(fifteen, 0)
    wait_send(idx.at[pl.ds(0, 240)], 1)
    wait_block_sent(send_g, G)
    wait_block_sent(send_r, R)
    wait_send(ft.at[:, :, pl.ds(0, 128)], 10)
    wait_send(at.at[:, :, pl.ds(0, 128)], 11)
    wait_send(d2.at[pl.ds(0, 128)], 12)
    wait_send(d1.at[pl.ds(0, 128)], 14)
    wait_send(ra, 15)
    wait_send(rb, 16)
    wait_send(ua, 24)
    wait_send(ub, 25)
    wait_send(r2a, 18)
    wait_send(r2b, 19)
    wait_send(r3a, 21)
    wait_send(r3b, 22)
    wait_send(hbuf.at[pl.ds(10, 7)], 23)


def deliver(node_in, small_in, score_out, node_out, first_out, second_out, head_out, held, small, sem_in, sem_out):
    spans = [pl.ds(i * 96, 96) for i in range(4)]
    ins = [pltpu.make_async_copy(node_in.at[p], held.at[p], sem_in.at[i]) for i, p in enumerate(spans)]
    outs = [pltpu.make_async_copy(held.at[p], node_out.at[p], sem_out.at[i]) for i, p in enumerate(spans)]
    rest = pltpu.make_async_copy(small_in, small, sem_in.at[4])
    for copy in ins + [rest]:
        copy.start()
    for i in range(4):
        ins[i].wait()
        outs[i].start()
    rest.wait()
    score_out[...] = small[13:14, 0:128].reshape(128)
    first_out[...] = small[0:8, :]
    second_out[...] = small[8:12, :]
    head_out[...] = small[12:13, :].reshape(HID)
    for copy in outs:
        copy.wait()


def shards(
    embeddings, endpoint_pairs, node_slot, first_weight, second_weight, score_weight, score_grad
):
    vm = pl.BlockSpec(memory_space=pltpu.VMEM)
    hbm = pl.BlockSpec(memory_space=pltpu.HBM)
    V = pltpu.VMEM
    scratch = [
        V((NODES // 128, 128), jnp.int32), V((ROWS, WIDTH), BF), V((2 * WIDTH, HID), BF), V((HID, HID), BF),
        V((HID, 2 * WIDTH), BF), V((HID, HID), BF),
        V((NDEV, 2 * EDGES), jnp.int32), V((4, NDEV, ROWS), BF), V((4, ROWS, NDEV), BF),
        V((4, 2, EDGES, 128), BF), V((4, 2, 128, EDGES), BF), V((2, 64 * 16, 128), F32),
        V((NDEV, 16, 256), BF), V((NDEV, 16, 256), BF), V((NDEV, 16, 256), BF), V((NDEV, 16, 256), BF),
        V((EDGES, 2 * WIDTH), BF), V((EDGES, HID), BF), V((EDGES, HID), F32),
        V((32, 2, 32, EDGES), BF), V((32, 32, 2 * EDGES), BF),
        V((32, 2, 16, EDGES), BF), V((32, 16, 2 * EDGES), BF),
        V((2 * EDGES, HID), BF), V((2 * EDGES, HID), BF), V((EDGES, 2 * WIDTH), BF),
        V((4, 4, 8, 16, 384), BF), V((4, 4, 8, 16, 384), BF),
        V((2, 4, 8, 16, 384), BF), V((2, 4, 8, 16, 384), BF),
        V((2, 2, 8, 16, 384), BF), V((2, 2, 8, 16, 384), BF),
        V((4, 8, 16, 384), BF), V((4, 8, 16, 384), BF),
        V((3, 8, 16, 384), BF), V((3, 8, 16, 384), BF),
        V((8, 16, 384), BF), V((8, 16, 384), BF),
        V((7, 16, 384), BF), V((7, 16, 384), BF),
        V((18, 1, HID), F32),
        V((15, 1, 2 * EDGES), jnp.int32),
        pltpu.SemaphoreType.DMA((4,)), pltpu.SemaphoreType.DMA((26,)), pltpu.SemaphoreType.DMA((26,)),
    ]
    node, small = pl.pallas_call(
        body,
        out_shape=(
            jax.ShapeDtypeStruct((ROWS, WIDTH), F32),
            jax.ShapeDtypeStruct((16, HID), F32),
        ),
        in_specs=[vm] * 3 + [hbm] * 4,
        out_specs=(vm, vm),
        scratch_shapes=scratch,
        compiler_params=pltpu.CompilerParams(
            collective_id=0, has_side_effects=True, vmem_limit_bytes=58 * 2**20
        ),
    )(
        endpoint_pairs.T, score_grad.reshape(1, EDGES), score_weight,
        node_slot.reshape(NODES // 128, 128), embeddings, first_weight, second_weight,
    )
    return pl.pallas_call(
        deliver,
        out_shape=(
            jax.ShapeDtypeStruct((EDGES,), F32),
            jax.ShapeDtypeStruct((ROWS, WIDTH), F32),
            jax.ShapeDtypeStruct((8, HID), F32),
            jax.ShapeDtypeStruct((4, HID), F32),
            jax.ShapeDtypeStruct((HID,), F32),
        ),
        in_specs=[hbm, hbm],
        out_specs=(vm, hbm, vm, vm, vm),
        scratch_shapes=[
            V((ROWS, WIDTH), F32), V((16, HID), F32), pltpu.SemaphoreType.DMA((5,)), pltpu.SemaphoreType.DMA((4,)),
        ],
    )(node, small)


def solution(mesh):
    both = P(("dom", "rep"))
    rows = P(("dom", "rep"), None)
    return jax.shard_map(
        shards,
        mesh=mesh,
        in_specs=(rows, rows, P(), P(), P(), P(), both),
        out_specs=(both, rows, rows, rows, P()),
        check_vma=False,
    )
```

```python
import functools

import jax
import jax.numpy as jnp
from jax import lax
from jax.experimental import pallas as pl
from jax.experimental.pallas import tpu as pltpu
from jax.sharding import PartitionSpec as P

MESH = pl.DeviceIdType.MESH
NY, NZ, NC, NX = 4, 8, 2, 4
NZC, NXY = NZ * NC, NX * NY
NDEV = NZC * NXY
NODES = 98304
ROWS, WIDTH, HID, EDGES = 384, 1024, 1024, 128
BF, F32 = jnp.bfloat16, jnp.float32
GELU_A, GELU_B = 0.7978845608028654, 0.044715


def dot(a, b):
    return jnp.dot(a, b, preferred_element_type=F32)


def dot_nt(a, b):
    return lax.dot_general(a, b, (((1,), (1,)), ((), ())), preferred_element_type=F32)


def dot_tn(a, b):
    return lax.dot_general(a, b, (((0,), (0,)), ((), ())), preferred_element_type=F32)


def gelu_both(v):
    t = jnp.tanh(GELU_A * (v + GELU_B * (v * v * v)))
    half = 0.5 * (1.0 + t)
    slope = half + 0.5 * v * (1.0 - t * t) * (GELU_A * (1.0 + (3.0 * GELU_B) * (v * v)))
    return v * half, slope


def iota(shape, dim):
    return lax.broadcasted_iota(jnp.int32, shape, dim)


def body(
    pairs, sgrad_in, sw_in, table_hbm, emb_hbm, w1_hbm, w2_hbm,
    node_out, small_out,
    table, emb, w1, w2, w1t, w2t, idx, hot, hot_t, picks, picks_t, stage,
    send_g, recv_g, send_r, recv_r,
    feats, first_act, first_slope, ft_own, ft, at_own, at, d1, d2, fg,
    pa, pb, ra, rb, ua, ub, sa, sb, r2a, r2b, ta, tb, r3a, r3b, hbuf,
    fifteen, load_sem, ss, rs,
):
    dom = lax.axis_index("dom")
    x = lax.axis_index("rep")
    y, z, c = dom // 16, (dom // 2) % 8, dom % 2
    zc = z * 2 + c
    xy = y * 4 + x
    me = xy * 16 + zc

    def ident(yy, zz, cc, xx):
        return ((yy * 8 + zz) * 2 + cc, xx)

    def zc_peer(k):
        return ident(y, (z + k % 8) % 8, (c + k // 8) % 2, x)

    def xy_peer(k):
        return ident((y + k // 4) % 4, z, c, (x + k % 4) % 4)

    def rcopy(src, dst, sem, dev):
        return pltpu.make_async_remote_copy(
            src_ref=src, dst_ref=dst, send_sem=ss.at[sem], recv_sem=rs.at[sem],
            device_id=dev, device_id_type=MESH,
        )

    def wait_send(ref, sem):
        pltpu.make_async_copy(ref, ref, ss.at[sem]).wait()

    def wait_recv(ref, sem):
        pltpu.make_async_copy(ref, ref, rs.at[sem]).wait()

    loads = [
        pltpu.make_async_copy(table_hbm, table, load_sem.at[0]),
        pltpu.make_async_copy(emb_hbm, emb, load_sem.at[1]),
        pltpu.make_async_copy(w1_hbm, w1, load_sem.at[2]),
        pltpu.make_async_copy(w2_hbm, w2, load_sem.at[3]),
    ]
    loads[0].start()
    bar = pltpu.get_barrier_semaphore()

    for k in range(1, 16):
        pl.semaphore_signal(bar, inc=1, device_id=zc_peer(k), device_id_type=MESH)
        pl.semaphore_signal(bar, inc=1, device_id=xy_peer(k), device_id_type=MESH)

    eye = iota((128, 128), 0) == iota((128, 128), 1)
    lanes = iota((128, 128), 1)
    loads[0].wait()
    for load in loads[1:]:
        load.start()
    slots = table[...]
    digits = jnp.concatenate(
        [(slots & 255).astype(F32), ((slots >> 8) & 255).astype(F32), (slots >> 16).astype(F32)], axis=1
    ).astype(BF)
    col_code, row_code = [], []
    for side in range(2):
        node_id = pairs[side:side + 1, :].astype(F32)
        node_id = jnp.sum(jnp.where(eye, node_id, 0.0), axis=1, keepdims=True).astype(jnp.int32)
        rows = ((node_id >> 7) == iota((128, NODES // 128), 1)).astype(F32).astype(BF)
        got = dot(rows, digits)
        slot = got[:, 0:128] + 256.0 * got[:, 128:256] + 65536.0 * got[:, 256:384]
        slot = jnp.sum(jnp.where(lanes == (node_id & 127), slot, 0.0), axis=1, keepdims=True)
        owner = ((slot + 0.5) * (1.0 / ROWS)).astype(jnp.int32)
        local = slot.astype(jnp.int32) - owner * ROWS
        quick = ((owner >> 6) * 4 + (owner & 3)) * 16 + ((owner >> 2) & 15)
        code = quick * 512 + local
        row = jnp.sum(jnp.where(eye, code.astype(F32), 0.0), axis=0, keepdims=True).astype(jnp.int32)
        col_code.append(code)
        row_code.append(row)

    idx[pl.ds(me, 1), :] = jnp.concatenate(row_code, axis=1)
    pl.semaphore_wait(bar, 30)

    for k in range(1, 16):
        row = idx.at[pl.ds(me, 1)]
        rcopy(row, row, 0, zc_peer(k)).start()

    wait_recv(fifteen, 0)

    for k in range(1, 16):
        rows = idx.at[pl.ds(xy * 16, 16)]
        rcopy(rows, rows, 1, xy_peer(k)).start()

    wait_recv(idx.at[pl.ds(0, 240)], 1)

    before = (iota((128, 128), 0) < iota((128, 128), 1)).astype(F32).astype(BF)
    for side in range(2):
        codes = idx[:, side * 128:(side + 1) * 128]
        mine = (codes >> 9) == me
        rank = dot(mine.astype(F32).astype(BF), before)
        local = ((codes & 511) + 1).astype(F32)
        for k in range(2):
            s = side * 2 + k
            hit = mine & (rank == float(k))
            found = jnp.sum(jnp.where(hit, local, 0.0), axis=1, keepdims=True).astype(jnp.int32) - 1
            for b in range(4):
                hot[b, s * 64:(s + 1) * 64, :] = (
                    (found[b * 64:(b + 1) * 64] == iota((64, ROWS), 1)).astype(F32).astype(BF)
                )

    def spread(s, n, part):
        for h in range(2):
            stage[h, pl.ds(s * 4 + n, 64, stride=16), :] = part[:, h * 128:(h + 1) * 128]

    def pack(dst, b):
        @pl.loop(0, 4)
        def _(i):
            rows = pl.ds(i * 256, 256)
            both = jnp.concatenate([stage[0, rows, :], stage[1, rows, :]], axis=1)
            dst[pl.ds(b * 64 + i * 16, 16)] = both.astype(BF).reshape(16, 16, 256)

    def unpack(src, b):
        @pl.loop(0, 4)
        def _(i):
            rows = pl.ds(i * 256, 256)
            both = src[pl.ds(b * 64 + i * 16, 16)].reshape(256, 256).astype(F32)
            stage[0, rows, :] = both[:, :128]
            stage[1, rows, :] = both[:, 128:]

    def collect(ss, n):
        out = []
        for s in ss:
            rows = pl.ds(s * 4 + n, 64, stride=16)
            out.append(jnp.concatenate([stage[0, rows, :], stage[1, rows, :]], axis=1))
        return jnp.concatenate(out, axis=0).astype(BF)

    def send_pair(src, dst, p, sem, first=0, last=8):
        @pl.loop(first, last)
        def _(k):
            xx = (x + k % 4) % 4
            cc = (c + k // 4) % 2
            for j in (p, p + 2):
                yy = (y + j) % 4

                def push(zz):
                    to = (yy * 4 + xx) * 16 + zz * 2 + cc
                    rcopy(src.at[to], dst.at[me], sem + j, ident(yy, zz, cc, xx)).start()

                if j == 0:
                    @pl.when(k > 0)
                    def _():
                        push(z)
                else:
                    push(z)
                for i in range(1, 8):
                    push((z + i) % 8)

    def wait_block(dst, j, sem):
        @pl.when(j == 0)
        def _():
            wait_recv(dst.at[pl.ds(0, 63)], sem)

        @pl.when(j > 0)
        def _():
            wait_recv(dst.at[pl.ds(0, 64)], sem + j)

    def wait_block_sent(src, sem):
        wait_send(src.at[pl.ds(0, 63)], sem)
        for j in range(1, 4):
            wait_send(src.at[pl.ds(0, 64)], sem + j)

    G, R = 2, 6
    loads[1].wait()

    for p in range(2):
        @pl.loop(0, 2)
        def _(i):
            b = (y + p + 2 * i) % 4
            for n in range(4):
                part = dot(hot[b], emb[:, n * 256:(n + 1) * 256])
                for s in range(4):
                    spread(s, n, part[s * 64:(s + 1) * 64])
            pack(send_g, b)

        send_pair(send_g, recv_g, p, G)

    recv_g[me] = send_g[me]

    earlier = iota((128, 128), 1) < iota((128, 128), 0)
    for side in range(2):
        row_owner = row_code[side] >> 9
        col_owner = col_code[side] >> 9
        rank = jnp.sum(jnp.where((col_owner == row_owner) & earlier, 1.0, 0.0), axis=1, keepdims=True)
        for b in range(4):
            home = col_owner == b * 64 + (lanes & 63)
            pick = jnp.where(home & (rank == (lanes >> 6).astype(F32)), 1.0, 0.0)
            picks[b, side] = pick.astype(BF)
            picks_t[b, side] = pick.T.astype(BF)
    feats[...] = jnp.zeros_like(feats)

    @pl.loop(0, 4)
    def _(b):
        hot_t[b] = hot[b].T

    loads[2].wait()
    loads[3].wait()

    @pl.loop(0, 8)
    def _(i):
        rows = pl.ds(pl.multiple_of(i * 256, 256), 256)
        for n in range(4):
            w1t[n * 256:(n + 1) * 256, rows] = w1[rows, n * 256:(n + 1) * 256].T

    @pl.loop(0, 4)
    def _(i):
        rows = pl.ds(pl.multiple_of(i * 256, 256), 256)
        for n in range(4):
            w2t[n * 256:(n + 1) * 256, rows] = w2[rows, n * 256:(n + 1) * 256].T

    @pl.loop(0, 4)
    def _(i):
        j = i % 2 * 2 + i // 2
        b = (y + 4 - j) % 4
        wait_block(recv_g, j, G)
        unpack(recv_g, b)
        for side in range(2):
            for n in range(4):
                cols = slice(side * 1024 + n * 256, side * 1024 + (n + 1) * 256)
                part = dot(picks[b, side], collect((side * 2, side * 2 + 1), n))
                feats[:, cols] = feats[:, cols] + part.astype(BF)

    other = ident(y, z, 1 - c, x)
    for n in range(4):
        cols = slice(n * 256, (n + 1) * 256)
        act, slope = gelu_both(dot(feats[...], w1[:, cols]))
        act = act.astype(BF)
        first_act[:, cols] = act
        first_slope[:, cols] = slope

    score = jnp.zeros((1, 128), F32)
    sgrad = jnp.sum(jnp.where(eye, sgrad_in[...], 0.0), axis=1, keepdims=True)
    for n in range(4):
        cols = slice(n * 256, (n + 1) * 256)
        act, slope = gelu_both(dot(first_act[...], w2[:, cols]))
        act = act.astype(BF)
        sw = sw_in[cols].reshape(1, 256)
        score += dot_nt(jnp.broadcast_to(sw, (8, 256)), act)[0:1]
        hbuf[0, :, cols] = jnp.sum(sgrad * act.astype(F32), axis=0, keepdims=True)
        d2[0:128, cols] = (sgrad * sw.astype(F32) * slope).astype(BF)
    small_out[13:14, 0:128] = score
    rcopy(d2.at[pl.ds(0, 128)], d2.at[pl.ds(128, 128)], 12, other).start()
    rcopy(hbuf.at[0], hbuf.at[1], 13, other).start()

    for n in range(4):
        cols = slice(n * 256, (n + 1) * 256)
        back = dot(d2[0:128, :], w2t[:, cols])
        d1[0:128, cols] = (back * first_slope[:, cols]).astype(BF)
    rcopy(d1.at[pl.ds(0, 128)], d1.at[pl.ds(128, 128)], 14, other).start()

    for n in range(8):
        cols = slice(n * 256, (n + 1) * 256)
        fg[:, cols] = dot(d1[0:128, :], w1t[:, cols]).astype(BF)

    def return_pack(j):
        b = (y + j) % 4
        for side in range(2):
            for n in range(4):
                col = side * 1024 + n * 256
                part = dot(picks_t[b, side], fg[:, col:col + 256])
                for k in range(2):
                    spread(side * 2 + k, n, part[k * 64:(k + 1) * 64])
        pack(send_r, b)

    def return_pair(p):
        @pl.loop(0, 2)
        def _(i):
            return_pack(p + 2 * i)

    return_pair(0)
    send_pair(send_r, recv_r, 0, R, 0, 4)

    for i in range(4):
        cols = slice(i * 256, (i + 1) * 256)
        at_own[i * 8:(i + 1) * 8] = first_act[:, cols].T.reshape(8, 2, 16, 128)
    rcopy(at_own.at[:, 1 - c], at.at[:, :, pl.ds(128, 128)], 11, other).start()
    at[:, :, 0:128] = at_own[:, c]
    for i in range(8):
        cols = slice(i * 256, (i + 1) * 256)
        ft_own[i * 4:(i + 1) * 4] = feats[:, cols].T.reshape(4, 2, 32, 128)
    rcopy(ft_own.at[:, 1 - c], ft.at[:, :, pl.ds(128, 128)], 10, other).start()
    ft[:, :, 0:128] = ft_own[:, c]

    wait_recv(at.at[:, :, pl.ds(0, 128)], 11)
    wait_recv(d2.at[pl.ds(0, 128)], 12)
    low = iota((8, 8, 512), 1) < 4

    @pl.loop(0, 4)
    def _(yy):
        res = dot(at[pl.ds(yy * 8, 8)].reshape(128, 256), d2[...]).reshape(8, 16, 1024)
        for pair in range(2):
            lo = res[:, pair * 8:(pair + 1) * 8, :512]
            hi = res[:, pair * 8:(pair + 1) * 8, 512:]
            even = jnp.where(low, lo, pltpu.roll(hi, 4, axis=1))
            odd = jnp.where(low, pltpu.roll(lo, 4, axis=1), hi)
            for bit, part in ((0, even), (1, odd)):
                full = jnp.concatenate([part[:, :, :256], part[:, :, 256:]], axis=1)
                pb[yy, pair * 2 + bit, :, :, 128:384] = full.astype(BF)

    wait_recv(ft.at[:, :, pl.ds(0, 128)], 10)
    wait_recv(d1.at[pl.ds(0, 128)], 14)

    @pl.loop(0, 4)
    def _(yy):
        lhs = ft[pl.ds(yy * 8, 8)].reshape(256, 256)
        for n in range(2):
            lo = dot(lhs, d1[:, n * 256:(n + 1) * 256]).reshape(8, 4, 8, 256)
            hi = dot(lhs, d1[:, 512 + n * 256:512 + (n + 1) * 256]).reshape(8, 4, 8, 256)
            for xx in range(4):
                full = jnp.concatenate([lo[:, xx], hi[:, xx]], axis=1).astype(BF)
                if n == 0:
                    pa[xx, yy, :, :, 0:256] = full
                else:
                    pa[xx, yy, :, :, 256:384] = full[:, :, :128]
                    pb[yy, xx, :, :, 0:128] = full[:, :, 128:]

    def along(axis, k):
        if axis == "x":
            return ident(y, z, c, (x + k) % 4), (x + k) % 4
        if axis == "y":
            return ident((y + k) % 4, z, c, x), (y + k) % 4
        return ident(y, (z + k) % 8, c, x), (z + k) % 8

    near, far = pl.ds(0, 2), pl.ds(2, 2)
    stages = (("x", x, pa, ra, ua, 15), ("y", y, pb, rb, ub, 16))
    for axis, mine, buf, got, aug, sem in stages:
        right, to_right = along(axis, 1)
        left, to_left = along(axis, 3)
        opposite = (mine + 2) % 4
        rcopy(buf.at[opposite, near], aug.at[0], sem + 9, right).start()
        rcopy(buf.at[opposite, far], aug.at[1], sem + 9, left).start()
        rcopy(buf.at[to_right, far], got.at[0, far], sem, right).start()
        rcopy(buf.at[to_left, near], got.at[1, near], sem, left).start()

    def head_step(base, count, axis, mine, sem):
        for k in range(1, count):
            dev, _ = along(axis, k)
            rcopy(hbuf.at[base + mine], hbuf.at[base + mine], sem, dev).start()

    wait_recv(hbuf.at[0], 13)
    wait_send(hbuf.at[0], 13)
    hbuf[2 + x] = hbuf[0] + hbuf[1]
    head_step(2, 4, "x", x, 17)

    send_pair(send_r, recv_r, 0, R, 4, 8)
    return_pair(1)

    for axis, mine, buf, got, aug, sem in stages:
        right, to_right = along(axis, 1)
        left, to_left = along(axis, 3)
        wait_recv(aug, sem + 9)

        @pl.loop(0, 2)
        def _(i):
            buf[to_right, i] = (buf[to_right, i].astype(F32) + aug[0, i].astype(F32)).astype(BF)
            buf[to_left, 2 + i] = (buf[to_left, 2 + i].astype(F32) + aug[1, i].astype(F32)).astype(BF)

        rcopy(buf.at[to_right, near], got.at[0, near], sem, right).start()
        rcopy(buf.at[to_left, far], got.at[1, far], sem, left).start()

    wait_recv(hbuf.at[pl.ds(2, 3)], 17)
    wait_send(hbuf.at[pl.ds(2, 3)], 17)
    hbuf[6 + y] = hbuf[2] + hbuf[3] + hbuf[4] + hbuf[5]
    head_step(6, 4, "y", y, 20)

    send_pair(send_r, recv_r, 1, R, 0, 4)

    node_out[...] = jnp.zeros_like(node_out)

    def land_block(j):
        b = (y + 4 - j) % 4
        wait_block(recv_r, j, R)
        unpack(recv_r, b)
        for n in range(4):
            cols = slice(n * 256, (n + 1) * 256)
            node_out[:, cols] = node_out[:, cols] + dot(hot_t[b], collect((0, 1, 2, 3), n))

    def add3(own, got, out, sec):
        total = own[sec].astype(F32) + got[0, sec].astype(F32) + got[1, sec].astype(F32)
        out[sec] = total.astype(BF)

    wait_recv(ra, 15)

    @pl.loop(0, 4)
    def _(i):
        add3(pa.at[x], ra, sa, i)

    for k in range(1, 4):
        dev, at_y = along("y", k)
        rcopy(sa.at[at_y], r2a.at[k - 1], 18, dev).start()
    wait_recv(rb, 16)

    @pl.loop(0, 4)
    def _(i):
        add3(pb.at[y], rb, sb, i)

    for k in range(1, 4):
        dev, at_x = along("x", k)
        rcopy(sb.at[at_x], r2b.at[k - 1], 19, dev).start()

    send_pair(send_r, recv_r, 1, R, 4, 8)
    recv_r[me] = send_r[me]

    wait_recv(hbuf.at[pl.ds(6, 3)], 20)
    wait_send(hbuf.at[pl.ds(6, 3)], 20)
    hbuf[10 + z] = hbuf[6] + hbuf[7] + hbuf[8] + hbuf[9]
    head_step(10, 8, "z", z, 23)

    @pl.loop(0, 1)
    def _(j):
        land_block(j)

    wait_recv(r2a, 18)
    total = sa[y].astype(F32) + r2a[0].astype(F32) + r2a[1].astype(F32) + r2a[2].astype(F32)
    ta[...] = total.astype(BF)
    for k in range(1, 8):
        dev, at_z = along("z", k)
        rcopy(ta.at[at_z], r3a.at[k - 1], 21, dev).start()
    wait_recv(r2b, 19)
    total = sb[x].astype(F32) + r2b[0].astype(F32) + r2b[1].astype(F32) + r2b[2].astype(F32)
    tb[...] = total.astype(BF)
    for k in range(1, 8):
        dev, at_z = along("z", k)
        rcopy(tb.at[at_z], r3b.at[k - 1], 22, dev).start()

    @pl.loop(2, 3)
    def _(j):
        land_block(j)

    wait_recv(r3a, 21)
    wait_recv(r3b, 22)
    left = ta[z].astype(F32)
    right = tb[z].astype(F32)
    for k in range(7):
        left += r3a[k].astype(F32)
        right += r3b[k].astype(F32)
    whole = jnp.concatenate([left, right], axis=1)
    small_out[0:8, 0:512] = whole[0:8, 0:512]
    small_out[0:8, 512:1024] = whole[8:16, 0:512]
    small_out[8:12, 0:256] = whole[0:4, 512:768]
    small_out[8:12, 512:768] = whole[4:8, 512:768]
    small_out[8:12, 256:512] = whole[8:12, 512:768]
    small_out[8:12, 768:1024] = whole[12:16, 512:768]

    wait_recv(hbuf.at[pl.ds(10, 7)], 23)
    head = hbuf[10]
    for k in range(1, 8):
        head += hbuf[10 + k]
    small_out[12:13, :] = head

    @pl.loop(0, 2)
    def _(i):
        land_block(1 + 2 * i)

    wait_send(fifteen, 0)
    wait_send(idx.at[pl.ds(0, 240)], 1)
    wait_block_sent(send_g, G)
    wait_block_sent(send_r, R)
    wait_send(ft.at[:, :, pl.ds(0, 128)], 10)
    wait_send(at.at[:, :, pl.ds(0, 128)], 11)
    wait_send(d2.at[pl.ds(0, 128)], 12)
    wait_send(d1.at[pl.ds(0, 128)], 14)
    wait_send(ra, 15)
    wait_send(rb, 16)
    wait_send(ua, 24)
    wait_send(ub, 25)
    wait_send(r2a, 18)
    wait_send(r2b, 19)
    wait_send(r3a, 21)
    wait_send(r3b, 22)
    wait_send(hbuf.at[pl.ds(10, 7)], 23)


def deliver(node_in, small_in, score_out, node_out, first_out, second_out, head_out, held, small, sem_in, sem_out):
    spans = [pl.ds(i * 96, 96) for i in range(4)]
    ins = [pltpu.make_async_copy(node_in.at[p], held.at[p], sem_in.at[i]) for i, p in enumerate(spans)]
    outs = [pltpu.make_async_copy(held.at[p], node_out.at[p], sem_out.at[i]) for i, p in enumerate(spans)]
    rest = pltpu.make_async_copy(small_in, small, sem_in.at[4])
    for copy in ins + [rest]:
        copy.start()
    for i in range(4):
        ins[i].wait()
        outs[i].start()
    rest.wait()
    score_out[...] = small[13:14, 0:128].reshape(128)
    first_out[...] = small[0:8, :]
    second_out[...] = small[8:12, :]
    head_out[...] = small[12:13, :].reshape(HID)
    for copy in outs:
        copy.wait()


def shards(
    embeddings, endpoint_pairs, node_slot, first_weight, second_weight, score_weight, score_grad
):
    vm = pl.BlockSpec(memory_space=pltpu.VMEM)
    hbm = pl.BlockSpec(memory_space=pltpu.HBM)
    V = pltpu.VMEM
    scratch = [
        V((NODES // 128, 128), jnp.int32), V((ROWS, WIDTH), BF), V((2 * WIDTH, HID), BF), V((HID, HID), BF),
        V((HID, 2 * WIDTH), BF), V((HID, HID), BF),
        V((NDEV, 2 * EDGES), jnp.int32), V((4, NDEV, ROWS), BF), V((4, ROWS, NDEV), BF),
        V((4, 2, EDGES, 128), BF), V((4, 2, 128, EDGES), BF), V((2, 64 * 16, 128), F32),
        V((NDEV, 16, 256), BF), V((NDEV, 16, 256), BF), V((NDEV, 16, 256), BF), V((NDEV, 16, 256), BF),
        V((EDGES, 2 * WIDTH), BF), V((EDGES, HID), BF), V((EDGES, HID), F32),
        V((32, 2, 32, EDGES), BF), V((32, 32, 2 * EDGES), BF),
        V((32, 2, 16, EDGES), BF), V((32, 16, 2 * EDGES), BF),
        V((2 * EDGES, HID), BF), V((2 * EDGES, HID), BF), V((EDGES, 2 * WIDTH), BF),
        V((4, 4, 8, 16, 384), BF), V((4, 4, 8, 16, 384), BF),
        V((2, 4, 8, 16, 384), BF), V((2, 4, 8, 16, 384), BF),
        V((2, 2, 8, 16, 384), BF), V((2, 2, 8, 16, 384), BF),
        V((4, 8, 16, 384), BF), V((4, 8, 16, 384), BF),
        V((3, 8, 16, 384), BF), V((3, 8, 16, 384), BF),
        V((8, 16, 384), BF), V((8, 16, 384), BF),
        V((7, 16, 384), BF), V((7, 16, 384), BF),
        V((18, 1, HID), F32),
        V((15, 1, 2 * EDGES), jnp.int32),
        pltpu.SemaphoreType.DMA((4,)), pltpu.SemaphoreType.DMA((26,)), pltpu.SemaphoreType.DMA((26,)),
    ]
    node, small = pl.pallas_call(
        body,
        out_shape=(
            jax.ShapeDtypeStruct((ROWS, WIDTH), F32),
            jax.ShapeDtypeStruct((16, HID), F32),
        ),
        in_specs=[vm] * 3 + [hbm] * 4,
        out_specs=(vm, vm),
        scratch_shapes=scratch,
        compiler_params=pltpu.CompilerParams(
            collective_id=0, has_side_effects=True, vmem_limit_bytes=58 * 2**20
        ),
    )(
        endpoint_pairs.T, score_grad.reshape(1, EDGES), score_weight,
        node_slot.reshape(NODES // 128, 128), embeddings, first_weight, second_weight,
    )
    return pl.pallas_call(
        deliver,
        out_shape=(
            jax.ShapeDtypeStruct((EDGES,), F32),
            jax.ShapeDtypeStruct((ROWS, WIDTH), F32),
            jax.ShapeDtypeStruct((8, HID), F32),
            jax.ShapeDtypeStruct((4, HID), F32),
            jax.ShapeDtypeStruct((HID,), F32),
        ),
        in_specs=[hbm, hbm],
        out_specs=(vm, hbm, vm, vm, vm),
        scratch_shapes=[
            V((ROWS, WIDTH), F32), V((16, HID), F32), pltpu.SemaphoreType.DMA((5,)), pltpu.SemaphoreType.DMA((4,)),
        ],
    )(node, small)


def solution(mesh):
    both = P(("dom", "rep"))
    rows = P(("dom", "rep"), None)
    return jax.shard_map(
        shards,
        mesh=mesh,
        in_specs=(rows, rows, P(), P(), P(), P(), both),
        out_specs=(both, rows, rows, rows, P()),
        check_vma=False,
    )
```

```python
import functools

import jax
import jax.numpy as jnp
from jax import lax
from jax.experimental import pallas as pl
from jax.experimental.pallas import tpu as pltpu
from jax.sharding import PartitionSpec as P

MESH = pl.DeviceIdType.MESH
NY, NZ, NC, NX = 4, 8, 2, 4
NZC, NXY = NZ * NC, NX * NY
NDEV = NZC * NXY
NODES = 98304
ROWS, WIDTH, HID, EDGES = 384, 1024, 1024, 128
BF, F32 = jnp.bfloat16, jnp.float32
GELU_A, GELU_B = 0.7978845608028654, 0.044715


def dot(a, b):
    return jnp.dot(a, b, preferred_element_type=F32)


def dot_nt(a, b):
    return lax.dot_general(a, b, (((1,), (1,)), ((), ())), preferred_element_type=F32)


def dot_tn(a, b):
    return lax.dot_general(a, b, (((0,), (0,)), ((), ())), preferred_element_type=F32)


def gelu_both(v):
    t = jnp.tanh(GELU_A * (v + GELU_B * (v * v * v)))
    half = 0.5 * (1.0 + t)
    slope = half + 0.5 * v * (1.0 - t * t) * (GELU_A * (1.0 + (3.0 * GELU_B) * (v * v)))
    return v * half, slope


def iota(shape, dim):
    return lax.broadcasted_iota(jnp.int32, shape, dim)


def body(
    pairs, sgrad_in, sw_in, table_hbm, emb_hbm, w1_hbm, w2_hbm,
    node_out, small_out,
    table, emb, w1, w2, w1t, w2t, idx, hot, hot_t, picks, picks_t, stage,
    send_g, recv_g, send_r, recv_r,
    feats, first_act, first_slope, ft_own, ft, at_own, at, d1, d2, fg,
    pa, pb, ra, rb, ua, ub, sa, sb, r2a, r2b, ta, tb, r3a, r3b, hbuf, node, second_act,
    fifteen, load_sem, ss, rs,
):
    dom = lax.axis_index("dom")
    x = lax.axis_index("rep")
    y, z, c = dom // 16, (dom // 2) % 8, dom % 2
    zc = z * 2 + c
    xy = y * 4 + x
    me = xy * 16 + zc

    def ident(yy, zz, cc, xx):
        return ((yy * 8 + zz) * 2 + cc, xx)

    def zc_peer(k):
        return ident(y, (z + k % 8) % 8, (c + k // 8) % 2, x)

    def xy_peer(k):
        return ident((y + k // 4) % 4, z, c, (x + k % 4) % 4)

    def rcopy(src, dst, sem, dev):
        return pltpu.make_async_remote_copy(
            src_ref=src, dst_ref=dst, send_sem=ss.at[sem], recv_sem=rs.at[sem],
            device_id=dev, device_id_type=MESH,
        )

    def wait_send(ref, sem):
        pltpu.make_async_copy(ref, ref, ss.at[sem]).wait()

    def wait_recv(ref, sem):
        pltpu.make_async_copy(ref, ref, rs.at[sem]).wait()

    loads = [
        pltpu.make_async_copy(table_hbm, table, load_sem.at[0]),
        pltpu.make_async_copy(emb_hbm, emb, load_sem.at[1]),
        pltpu.make_async_copy(w1_hbm, w1, load_sem.at[2]),
        pltpu.make_async_copy(w2_hbm, w2, load_sem.at[3]),
    ]
    loads[0].start()
    bar = pltpu.get_barrier_semaphore()

    for k in range(1, 16):
        pl.semaphore_signal(bar, inc=1, device_id=zc_peer(k), device_id_type=MESH)
        pl.semaphore_signal(bar, inc=1, device_id=xy_peer(k), device_id_type=MESH)

    eye = iota((128, 128), 0) == iota((128, 128), 1)
    lanes = iota((128, 128), 1)
    loads[0].wait()
    for load in loads[1:]:
        load.start()
    slots = table[...]
    digits = jnp.concatenate(
        [(slots & 255).astype(F32), ((slots >> 8) & 255).astype(F32), (slots >> 16).astype(F32)], axis=1
    ).astype(BF)
    col_code, row_code = [], []
    for side in range(2):
        node_id = pairs[side:side + 1, :].astype(F32)
        node_id = jnp.sum(jnp.where(eye, node_id, 0.0), axis=1, keepdims=True).astype(jnp.int32)
        rows = ((node_id >> 7) == iota((128, NODES // 128), 1)).astype(F32).astype(BF)
        got = dot(rows, digits)
        slot = got[:, 0:128] + 256.0 * got[:, 128:256] + 65536.0 * got[:, 256:384]
        slot = jnp.sum(jnp.where(lanes == (node_id & 127), slot, 0.0), axis=1, keepdims=True)
        owner = ((slot + 0.5) * (1.0 / ROWS)).astype(jnp.int32)
        local = slot.astype(jnp.int32) - owner * ROWS
        quick = ((owner >> 6) * 4 + (owner & 3)) * 16 + ((owner >> 2) & 15)
        code = quick * 512 + local
        row = jnp.sum(jnp.where(eye, code.astype(F32), 0.0), axis=0, keepdims=True).astype(jnp.int32)
        col_code.append(code)
        row_code.append(row)

    idx[pl.ds(me, 1), :] = jnp.concatenate(row_code, axis=1)
    pl.semaphore_wait(bar, 30)

    for k in range(1, 16):
        row = idx.at[pl.ds(me, 1)]
        rcopy(row, row, 0, zc_peer(k)).start()

    wait_recv(fifteen, 0)

    for k in range(1, 16):
        rows = idx.at[pl.ds(xy * 16, 16)]
        rcopy(rows, rows, 1, xy_peer(k)).start()

    wait_recv(idx.at[pl.ds(0, 240)], 1)

    before = (iota((128, 128), 0) < iota((128, 128), 1)).astype(F32).astype(BF)
    for side in range(2):
        codes = idx[:, side * 128:(side + 1) * 128]
        mine = (codes >> 9) == me
        rank = dot(mine.astype(F32).astype(BF), before)
        local = ((codes & 511) + 1).astype(F32)
        for k in range(2):
            s = side * 2 + k
            hit = mine & (rank == float(k))
            found = jnp.sum(jnp.where(hit, local, 0.0), axis=1, keepdims=True).astype(jnp.int32) - 1
            for b in range(4):
                hot[b, s * 64:(s + 1) * 64, :] = (
                    (found[b * 64:(b + 1) * 64] == iota((64, ROWS), 1)).astype(F32).astype(BF)
                )

    def spread(s, n, part):
        for h in range(2):
            stage[h, pl.ds(s * 4 + n, 64, stride=16), :] = part[:, h * 128:(h + 1) * 128]

    def pack(dst, b):
        @pl.loop(0, 4)
        def _(i):
            rows = pl.ds(i * 256, 256)
            both = jnp.concatenate([stage[0, rows, :], stage[1, rows, :]], axis=1)
            dst[pl.ds(b * 64 + i * 16, 16)] = both.astype(BF).reshape(16, 16, 256)

    def unpack(src, b):
        @pl.loop(0, 4)
        def _(i):
            rows = pl.ds(i * 256, 256)
            both = src[pl.ds(b * 64 + i * 16, 16)].reshape(256, 256).astype(F32)
            stage[0, rows, :] = both[:, :128]
            stage[1, rows, :] = both[:, 128:]

    def collect(ss, n):
        out = []
        for s in ss:
            rows = pl.ds(s * 4 + n, 64, stride=16)
            out.append(jnp.concatenate([stage[0, rows, :], stage[1, rows, :]], axis=1))
        return jnp.concatenate(out, axis=0).astype(BF)

    def send_pair(src, dst, p, sem, first=0, last=8):
        @pl.loop(first, last)
        def _(k):
            cc = (c + k // 4) % 2
            for j in (p, p + 2):
                yy = (y + j) % 4
                xx = (x + (k + j - p) % 4) % 4

                def push(zz):
                    to = (yy * 4 + xx) * 16 + zz * 2 + cc
                    rcopy(src.at[to], dst.at[me], sem + j, ident(yy, zz, cc, xx)).start()

                if j == 0:
                    @pl.when(k > 0)
                    def _():
                        push(z)
                else:
                    push(z)
                for i in range(1, 8):
                    push((z + i) % 8)

    def wait_block(dst, j, sem):
        @pl.when(j == 0)
        def _():
            wait_recv(dst.at[pl.ds(0, 63)], sem)

        @pl.when(j > 0)
        def _():
            wait_recv(dst.at[pl.ds(0, 64)], sem + j)

    def wait_block_sent(src, sem):
        wait_send(src.at[pl.ds(0, 63)], sem)
        for j in range(1, 4):
            wait_send(src.at[pl.ds(0, 64)], sem + j)

    G, R = 2, 6
    loads[1].wait()

    for p in range(2):
        @pl.loop(0, 2)
        def _(i):
            b = (y + p + 2 * i) % 4
            for n in range(4):
                part = dot(hot[b], emb[:, n * 256:(n + 1) * 256])
                for s in range(4):
                    spread(s, n, part[s * 64:(s + 1) * 64])
            pack(send_g, b)

        send_pair(send_g, recv_g, p, G)

    recv_g[me] = send_g[me]

    earlier = iota((128, 128), 1) < iota((128, 128), 0)
    for side in range(2):
        row_owner = row_code[side] >> 9
        col_owner = col_code[side] >> 9
        rank = jnp.sum(jnp.where((col_owner == row_owner) & earlier, 1.0, 0.0), axis=1, keepdims=True)
        for b in range(4):
            home = col_owner == b * 64 + (lanes & 63)
            pick = jnp.where(home & (rank == (lanes >> 6).astype(F32)), 1.0, 0.0)
            picks[b, side] = pick.astype(BF)
            picks_t[b, side] = pick.T.astype(BF)
    feats[...] = jnp.zeros_like(feats)

    @pl.loop(0, 4)
    def _(b):
        hot_t[b] = hot[b].T

    loads[2].wait()
    loads[3].wait()

    @pl.loop(0, 8)
    def _(i):
        rows = pl.ds(pl.multiple_of(i * 256, 256), 256)
        for n in range(4):
            w1t[n * 256:(n + 1) * 256, rows] = w1[rows, n * 256:(n + 1) * 256].T

    @pl.loop(0, 4)
    def _(i):
        rows = pl.ds(pl.multiple_of(i * 256, 256), 256)
        for n in range(4):
            w2t[n * 256:(n + 1) * 256, rows] = w2[rows, n * 256:(n + 1) * 256].T

    @pl.loop(0, 4)
    def _(i):
        j = i % 2 * 2 + i // 2
        b = (y + 4 - j) % 4
        wait_block(recv_g, j, G)
        unpack(recv_g, b)
        for side in range(2):
            for n in range(4):
                cols = slice(side * 1024 + n * 256, side * 1024 + (n + 1) * 256)
                part = dot(picks[b, side], collect((side * 2, side * 2 + 1), n))
                feats[:, cols] = feats[:, cols] + part.astype(BF)

    other = ident(y, z, 1 - c, x)
    for n in range(4):
        cols = slice(n * 256, (n + 1) * 256)
        act, slope = gelu_both(dot(feats[...], w1[:, cols]))
        act = act.astype(BF)
        first_act[:, cols] = act
        first_slope[:, cols] = slope

    sgrad = jnp.sum(jnp.where(eye, sgrad_in[...], 0.0), axis=1, keepdims=True)
    for n in range(4):
        cols = slice(n * 256, (n + 1) * 256)
        act, slope = gelu_both(dot(first_act[...], w2[:, cols]))
        act = act.astype(BF)
        sw = sw_in[cols].reshape(1, 256)
        second_act[:, cols] = act
        d2[0:128, cols] = (sgrad * sw.astype(F32) * slope).astype(BF)
    rcopy(d2.at[pl.ds(0, 128)], d2.at[pl.ds(128, 128)], 12, other).start()

    for n in range(4):
        cols = slice(n * 256, (n + 1) * 256)
        back = dot(d2[0:128, :], w2t[:, cols])
        d1[0:128, cols] = (back * first_slope[:, cols]).astype(BF)
    rcopy(d1.at[pl.ds(0, 128)], d1.at[pl.ds(128, 128)], 14, other).start()

    for n in range(8):
        cols = slice(n * 256, (n + 1) * 256)
        fg[:, cols] = dot(d1[0:128, :], w1t[:, cols]).astype(BF)

    def return_pack(j):
        b = (y + j) % 4
        for side in range(2):
            for n in range(4):
                col = side * 1024 + n * 256
                part = dot(picks_t[b, side], fg[:, col:col + 256])
                for k in range(2):
                    spread(side * 2 + k, n, part[k * 64:(k + 1) * 64])
        pack(send_r, b)

    def return_pair(p):
        @pl.loop(0, 2)
        def _(i):
            return_pack(p + 2 * i)

    return_pair(0)
    send_pair(send_r, recv_r, 0, R, 0, 4)

    score = jnp.zeros((1, 128), F32)
    for n in range(4):
        cols = slice(n * 256, (n + 1) * 256)
        act = second_act[:, cols]
        hbuf[0, :, cols] = jnp.sum(sgrad * act.astype(F32), axis=0, keepdims=True)
        score += dot_nt(jnp.broadcast_to(sw_in[cols].reshape(1, 256), (8, 256)), act)[0:1]
    small_out[13:14, 0:128] = score
    rcopy(hbuf.at[0], hbuf.at[1], 13, other).start()

    for i in range(4):
        cols = slice(i * 256, (i + 1) * 256)
        at_own[i * 8:(i + 1) * 8] = first_act[:, cols].T.reshape(8, 2, 16, 128)
    rcopy(at_own.at[:, 1 - c], at.at[:, :, pl.ds(128, 128)], 11, other).start()
    at[:, :, 0:128] = at_own[:, c]
    for i in range(8):
        cols = slice(i * 256, (i + 1) * 256)
        ft_own[i * 4:(i + 1) * 4] = feats[:, cols].T.reshape(4, 2, 32, 128)
    rcopy(ft_own.at[:, 1 - c], ft.at[:, :, pl.ds(128, 128)], 10, other).start()
    ft[:, :, 0:128] = ft_own[:, c]

    wait_recv(at.at[:, :, pl.ds(0, 128)], 11)
    wait_recv(d2.at[pl.ds(0, 128)], 12)
    low = iota((8, 8, 512), 1) < 4

    @pl.loop(0, 4)
    def _(yy):
        res = dot(at[pl.ds(yy * 8, 8)].reshape(128, 256), d2[...]).reshape(8, 16, 1024)
        for pair in range(2):
            lo = res[:, pair * 8:(pair + 1) * 8, :512]
            hi = res[:, pair * 8:(pair + 1) * 8, 512:]
            even = jnp.where(low, lo, pltpu.roll(hi, 4, axis=1))
            odd = jnp.where(low, pltpu.roll(lo, 4, axis=1), hi)
            for bit, part in ((0, even), (1, odd)):
                full = jnp.concatenate([part[:, :, :256], part[:, :, 256:]], axis=1)
                pb[yy, pair * 2 + bit, :, :, 128:384] = full.astype(BF)

    wait_recv(ft.at[:, :, pl.ds(0, 128)], 10)
    wait_recv(d1.at[pl.ds(0, 128)], 14)

    @pl.loop(0, 4)
    def _(yy):
        lhs = ft[pl.ds(yy * 8, 8)].reshape(256, 256)
        for n in range(2):
            lo = dot(lhs, d1[:, n * 256:(n + 1) * 256]).reshape(8, 4, 8, 256)
            hi = dot(lhs, d1[:, 512 + n * 256:512 + (n + 1) * 256]).reshape(8, 4, 8, 256)
            for xx in range(4):
                full = jnp.concatenate([lo[:, xx], hi[:, xx]], axis=1).astype(BF)
                if n == 0:
                    pa[xx, yy, :, :, 0:256] = full
                else:
                    pa[xx, yy, :, :, 256:384] = full[:, :, :128]
                    pb[yy, xx, :, :, 0:128] = full[:, :, 128:]

    def along(axis, k):
        if axis == "x":
            return ident(y, z, c, (x + k) % 4), (x + k) % 4
        if axis == "y":
            return ident((y + k) % 4, z, c, x), (y + k) % 4
        return ident(y, (z + k) % 8, c, x), (z + k) % 8

    near, far = pl.ds(0, 2), pl.ds(2, 2)
    stages = (("x", x, pa, ra, ua, 15), ("y", y, pb, rb, ub, 16))
    for axis, mine, buf, got, aug, sem in stages:
        right, to_right = along(axis, 1)
        left, to_left = along(axis, 3)
        opposite = (mine + 2) % 4
        rcopy(buf.at[opposite, near], aug.at[0], sem + 9, right).start()
        rcopy(buf.at[opposite, far], aug.at[1], sem + 9, left).start()
        rcopy(buf.at[to_right, far], got.at[0, far], sem, right).start()
        rcopy(buf.at[to_left, near], got.at[1, near], sem, left).start()

    def head_step(base, count, axis, mine, sem):
        for k in range(1, count):
            dev, _ = along(axis, k)
            rcopy(hbuf.at[base + mine], hbuf.at[base + mine], sem, dev).start()

    wait_recv(hbuf.at[0], 13)
    wait_send(hbuf.at[0], 13)
    hbuf[2 + x] = hbuf[0] + hbuf[1]
    head_step(2, 4, "x", x, 17)

    send_pair(send_r, recv_r, 0, R, 4, 8)
    return_pair(1)

    for axis, mine, buf, got, aug, sem in stages:
        right, to_right = along(axis, 1)
        left, to_left = along(axis, 3)
        wait_recv(aug, sem + 9)

        @pl.loop(0, 2)
        def _(i):
            buf[to_right, i] = (buf[to_right, i].astype(F32) + aug[0, i].astype(F32)).astype(BF)
            buf[to_left, 2 + i] = (buf[to_left, 2 + i].astype(F32) + aug[1, i].astype(F32)).astype(BF)

        rcopy(buf.at[to_right, near], got.at[0, near], sem, right).start()
        rcopy(buf.at[to_left, far], got.at[1, far], sem, left).start()

    wait_recv(hbuf.at[pl.ds(2, 3)], 17)
    wait_send(hbuf.at[pl.ds(2, 3)], 17)
    hbuf[6 + y] = hbuf[2] + hbuf[3] + hbuf[4] + hbuf[5]
    head_step(6, 4, "y", y, 20)

    send_pair(send_r, recv_r, 1, R, 0, 4)

    node[...] = jnp.zeros_like(node)

    def land_block(j):
        b = (y + 4 - j) % 4
        wait_block(recv_r, j, R)
        unpack(recv_r, b)
        for n in range(4):
            cols = slice(n * 256, (n + 1) * 256)
            node[:, cols] = node[:, cols] + dot(hot_t[b], collect((0, 1, 2, 3), n))

    def add3(own, got, out, sec):
        total = own[sec].astype(F32) + got[0, sec].astype(F32) + got[1, sec].astype(F32)
        out[sec] = total.astype(BF)

    wait_recv(ra, 15)

    @pl.loop(0, 4)
    def _(i):
        add3(pa.at[x], ra, sa, i)

    for k in range(1, 4):
        dev, at_y = along("y", k)
        rcopy(sa.at[at_y], r2a.at[k - 1], 18, dev).start()
    wait_recv(rb, 16)

    @pl.loop(0, 4)
    def _(i):
        add3(pb.at[y], rb, sb, i)

    for k in range(1, 4):
        dev, at_x = along("x", k)
        rcopy(sb.at[at_x], r2b.at[k - 1], 19, dev).start()

    send_pair(send_r, recv_r, 1, R, 4, 8)
    recv_r[me] = send_r[me]

    wait_recv(hbuf.at[pl.ds(6, 3)], 20)
    wait_send(hbuf.at[pl.ds(6, 3)], 20)
    hbuf[10 + z] = hbuf[6] + hbuf[7] + hbuf[8] + hbuf[9]
    head_step(10, 8, "z", z, 23)

    @pl.loop(0, 1)
    def _(j):
        land_block(j)

    wait_recv(r2a, 18)
    total = sa[y].astype(F32) + r2a[0].astype(F32) + r2a[1].astype(F32) + r2a[2].astype(F32)
    ta[...] = total.astype(BF)
    for k in range(1, 8):
        dev, at_z = along("z", k)
        rcopy(ta.at[at_z], r3a.at[k - 1], 21, dev).start()
    wait_recv(r2b, 19)
    total = sb[x].astype(F32) + r2b[0].astype(F32) + r2b[1].astype(F32) + r2b[2].astype(F32)
    tb[...] = total.astype(BF)
    for k in range(1, 8):
        dev, at_z = along("z", k)
        rcopy(tb.at[at_z], r3b.at[k - 1], 22, dev).start()

    @pl.loop(2, 3)
    def _(j):
        land_block(j)

    wait_recv(r3a, 21)
    wait_recv(r3b, 22)
    left = ta[z].astype(F32)
    right = tb[z].astype(F32)
    for k in range(7):
        left += r3a[k].astype(F32)
        right += r3b[k].astype(F32)
    whole = jnp.concatenate([left, right], axis=1)
    small_out[0:8, 0:512] = whole[0:8, 0:512]
    small_out[0:8, 512:1024] = whole[8:16, 0:512]
    small_out[8:12, 0:256] = whole[0:4, 512:768]
    small_out[8:12, 512:768] = whole[4:8, 512:768]
    small_out[8:12, 256:512] = whole[8:12, 512:768]
    small_out[8:12, 768:1024] = whole[12:16, 512:768]

    wait_recv(hbuf.at[pl.ds(10, 7)], 23)
    head = hbuf[10]
    for k in range(1, 8):
        head += hbuf[10 + k]
    small_out[12:13, :] = head

    land_block(1)
    b = (y + 1) % 4
    wait_block(recv_r, 3, R)
    unpack(recv_r, b)
    outs = []
    for n in range(4):
        cols = slice(n * 256, (n + 1) * 256)
        node[:, cols] = node[:, cols] + dot(hot_t[b], collect((0, 1, 2, 3), n))
        outs.append(pltpu.make_async_copy(node.at[:, cols], node_out.at[:, cols], load_sem.at[n]))
        outs[n].start()

    wait_send(fifteen, 0)
    wait_send(idx.at[pl.ds(0, 240)], 1)
    wait_block_sent(send_g, G)
    wait_block_sent(send_r, R)
    wait_send(ft.at[:, :, pl.ds(0, 128)], 10)
    wait_send(at.at[:, :, pl.ds(0, 128)], 11)
    wait_send(d2.at[pl.ds(0, 128)], 12)
    wait_send(d1.at[pl.ds(0, 128)], 14)
    wait_send(ra, 15)
    wait_send(rb, 16)
    wait_send(ua, 24)
    wait_send(ub, 25)
    wait_send(r2a, 18)
    wait_send(r2b, 19)
    wait_send(r3a, 21)
    wait_send(r3b, 22)
    wait_send(hbuf.at[pl.ds(10, 7)], 23)
    for out in outs:
        out.wait()


def deliver(node_in, small_in, score_out, node_out, first_out, second_out, head_out, held, small, sem_in, sem_out):
    spans = [pl.ds(i * 96, 96) for i in range(4)]
    ins = [pltpu.make_async_copy(node_in.at[p], held.at[p], sem_in.at[i]) for i, p in enumerate(spans)]
    outs = [pltpu.make_async_copy(held.at[p], node_out.at[p], sem_out.at[i]) for i, p in enumerate(spans)]
    rest = pltpu.make_async_copy(small_in, small, sem_in.at[4])
    for copy in ins + [rest]:
        copy.start()
    for i in range(4):
        ins[i].wait()
        outs[i].start()
    rest.wait()
    score_out[...] = small[13:14, 0:128].reshape(128)
    first_out[...] = small[0:8, :]
    second_out[...] = small[8:12, :]
    head_out[...] = small[12:13, :].reshape(HID)
    for copy in outs:
        copy.wait()


def shards(
    embeddings, endpoint_pairs, node_slot, first_weight, second_weight, score_weight, score_grad
):
    vm = pl.BlockSpec(memory_space=pltpu.VMEM)
    hbm = pl.BlockSpec(memory_space=pltpu.HBM)
    V = pltpu.VMEM
    scratch = [
        V((NODES // 128, 128), jnp.int32), V((ROWS, WIDTH), BF), V((2 * WIDTH, HID), BF), V((HID, HID), BF),
        V((HID, 2 * WIDTH), BF), V((HID, HID), BF),
        V((NDEV, 2 * EDGES), jnp.int32), V((4, NDEV, ROWS), BF), V((4, ROWS, NDEV), BF),
        V((4, 2, EDGES, 128), BF), V((4, 2, 128, EDGES), BF), V((2, 64 * 16, 128), F32),
        V((NDEV, 16, 256), BF), V((NDEV, 16, 256), BF), V((NDEV, 16, 256), BF), V((NDEV, 16, 256), BF),
        V((EDGES, 2 * WIDTH), BF), V((EDGES, HID), BF), V((EDGES, HID), F32),
        V((32, 2, 32, EDGES), BF), V((32, 32, 2 * EDGES), BF),
        V((32, 2, 16, EDGES), BF), V((32, 16, 2 * EDGES), BF),
        V((2 * EDGES, HID), BF), V((2 * EDGES, HID), BF), V((EDGES, 2 * WIDTH), BF),
        V((4, 4, 8, 16, 384), BF), V((4, 4, 8, 16, 384), BF),
        V((2, 4, 8, 16, 384), BF), V((2, 4, 8, 16, 384), BF),
        V((2, 2, 8, 16, 384), BF), V((2, 2, 8, 16, 384), BF),
        V((4, 8, 16, 384), BF), V((4, 8, 16, 384), BF),
        V((3, 8, 16, 384), BF), V((3, 8, 16, 384), BF),
        V((8, 16, 384), BF), V((8, 16, 384), BF),
        V((7, 16, 384), BF), V((7, 16, 384), BF),
        V((18, 1, HID), F32), V((ROWS, WIDTH), F32), V((EDGES, HID), BF),
        V((15, 1, 2 * EDGES), jnp.int32),
        pltpu.SemaphoreType.DMA((4,)), pltpu.SemaphoreType.DMA((26,)), pltpu.SemaphoreType.DMA((26,)),
    ]
    node, small = pl.pallas_call(
        body,
        out_shape=(
            jax.ShapeDtypeStruct((ROWS, WIDTH), F32),
            jax.ShapeDtypeStruct((16, HID), F32),
        ),
        in_specs=[vm] * 3 + [hbm] * 4,
        out_specs=(hbm, vm),
        scratch_shapes=scratch,
        compiler_params=pltpu.CompilerParams(
            collective_id=0, has_side_effects=True, vmem_limit_bytes=58 * 2**20
        ),
    )(
        endpoint_pairs.T, score_grad.reshape(1, EDGES), score_weight,
        node_slot.reshape(NODES // 128, 128), embeddings, first_weight, second_weight,
    )
    return pl.pallas_call(
        deliver,
        out_shape=(
            jax.ShapeDtypeStruct((EDGES,), F32),
            jax.ShapeDtypeStruct((ROWS, WIDTH), F32),
            jax.ShapeDtypeStruct((8, HID), F32),
            jax.ShapeDtypeStruct((4, HID), F32),
            jax.ShapeDtypeStruct((HID,), F32),
        ),
        in_specs=[hbm, hbm],
        out_specs=(vm, hbm, vm, vm, vm),
        scratch_shapes=[
            V((ROWS, WIDTH), F32), V((16, HID), F32), pltpu.SemaphoreType.DMA((5,)), pltpu.SemaphoreType.DMA((4,)),
        ],
    )(node, small)


def solution(mesh):
    both = P(("dom", "rep"))
    rows = P(("dom", "rep"), None)
    return jax.shard_map(
        shards,
        mesh=mesh,
        in_specs=(rows, rows, P(), P(), P(), P(), both),
        out_specs=(both, rows, rows, rows, P()),
        check_vma=False,
    )
```

```python
import functools

import jax
import jax.numpy as jnp
from jax import lax
from jax.experimental import pallas as pl
from jax.experimental.pallas import tpu as pltpu
from jax.sharding import PartitionSpec as P

MESH = pl.DeviceIdType.MESH
NY, NZ, NC, NX = 4, 8, 2, 4
NZC, NXY = NZ * NC, NX * NY
NDEV = NZC * NXY
NODES = 98304
ROWS, WIDTH, HID, EDGES = 384, 1024, 1024, 128
BF, F32 = jnp.bfloat16, jnp.float32
GELU_A, GELU_B = 0.7978845608028654, 0.044715


def dot(a, b):
    return jnp.dot(a, b, preferred_element_type=F32)


def dot_nt(a, b):
    return lax.dot_general(a, b, (((1,), (1,)), ((), ())), preferred_element_type=F32)


def dot_tn(a, b):
    return lax.dot_general(a, b, (((0,), (0,)), ((), ())), preferred_element_type=F32)


def gelu_both(v):
    t = jnp.tanh(GELU_A * (v + GELU_B * (v * v * v)))
    half = 0.5 * (1.0 + t)
    slope = half + 0.5 * v * (1.0 - t * t) * (GELU_A * (1.0 + (3.0 * GELU_B) * (v * v)))
    return v * half, slope


def iota(shape, dim):
    return lax.broadcasted_iota(jnp.int32, shape, dim)


def body(
    pairs, sgrad_in, sw_in, table_hbm, emb_hbm, w1_hbm, w2_hbm,
    node_out, small_out,
    table, emb, w1, w2, w1t, w2t, idx, hot, hot_t, picks, picks_t, stage,
    send_g, recv_g, send_r, recv_r,
    feats, first_act, first_slope, ft_own, ft, at_own, at, d1, d2, fg,
    pa, pb, ra, rb, sa, sb, r2a, r2b, ta, tb, r3a, r3b, hbuf, node, second_act,
    fifteen, load_sem, ss, rs,
):
    dom = lax.axis_index("dom")
    x = lax.axis_index("rep")
    y, z, c = dom // 16, (dom // 2) % 8, dom % 2
    zc = z * 2 + c
    xy = y * 4 + x
    me = xy * 16 + zc

    def ident(yy, zz, cc, xx):
        return ((yy * 8 + zz) * 2 + cc, xx)

    def zc_peer(k):
        return ident(y, (z + k % 8) % 8, (c + k // 8) % 2, x)

    def xy_peer(k):
        return ident((y + k // 4) % 4, z, c, (x + k % 4) % 4)

    def rcopy(src, dst, sem, dev):
        return pltpu.make_async_remote_copy(
            src_ref=src, dst_ref=dst, send_sem=ss.at[sem], recv_sem=rs.at[sem],
            device_id=dev, device_id_type=MESH,
        )

    def wait_send(ref, sem):
        pltpu.make_async_copy(ref, ref, ss.at[sem]).wait()

    def wait_recv(ref, sem):
        pltpu.make_async_copy(ref, ref, rs.at[sem]).wait()

    loads = [
        pltpu.make_async_copy(table_hbm, table, load_sem.at[0]),
        pltpu.make_async_copy(emb_hbm, emb, load_sem.at[1]),
        pltpu.make_async_copy(w1_hbm, w1, load_sem.at[2]),
        pltpu.make_async_copy(w2_hbm, w2, load_sem.at[3]),
    ]
    loads[0].start()
    bar = pltpu.get_barrier_semaphore()

    for k in range(1, 16):
        pl.semaphore_signal(bar, inc=1, device_id=zc_peer(k), device_id_type=MESH)
        pl.semaphore_signal(bar, inc=1, device_id=xy_peer(k), device_id_type=MESH)

    eye = iota((128, 128), 0) == iota((128, 128), 1)
    lanes = iota((128, 128), 1)
    loads[0].wait()
    for load in loads[1:]:
        load.start()
    slots = table[...]
    digits = jnp.concatenate(
        [(slots & 255).astype(F32), ((slots >> 8) & 255).astype(F32), (slots >> 16).astype(F32)], axis=1
    ).astype(BF)
    col_code, row_code = [], []
    for side in range(2):
        node_id = pairs[side:side + 1, :].astype(F32)
        node_id = jnp.sum(jnp.where(eye, node_id, 0.0), axis=1, keepdims=True).astype(jnp.int32)
        rows = ((node_id >> 7) == iota((128, NODES // 128), 1)).astype(F32).astype(BF)
        got = dot(rows, digits)
        slot = got[:, 0:128] + 256.0 * got[:, 128:256] + 65536.0 * got[:, 256:384]
        slot = jnp.sum(jnp.where(lanes == (node_id & 127), slot, 0.0), axis=1, keepdims=True)
        owner = ((slot + 0.5) * (1.0 / ROWS)).astype(jnp.int32)
        local = slot.astype(jnp.int32) - owner * ROWS
        quick = ((owner >> 6) * 4 + (owner & 3)) * 16 + ((owner >> 2) & 15)
        code = quick * 512 + local
        row = jnp.sum(jnp.where(eye, code.astype(F32), 0.0), axis=0, keepdims=True).astype(jnp.int32)
        col_code.append(code)
        row_code.append(row)

    idx[pl.ds(me, 1), :] = jnp.concatenate(row_code, axis=1)
    pl.semaphore_wait(bar, 30)

    for k in range(1, 16):
        row = idx.at[pl.ds(me, 1)]
        rcopy(row, row, 0, zc_peer(k)).start()

    wait_recv(fifteen, 0)

    for k in range(1, 16):
        rows = idx.at[pl.ds(xy * 16, 16)]
        rcopy(rows, rows, 1, xy_peer(k)).start()

    wait_recv(idx.at[pl.ds(0, 240)], 1)

    before = (iota((128, 128), 0) < iota((128, 128), 1)).astype(F32).astype(BF)
    for side in range(2):
        codes = idx[:, side * 128:(side + 1) * 128]
        mine = (codes >> 9) == me
        rank = dot(mine.astype(F32).astype(BF), before)
        local = ((codes & 511) + 1).astype(F32)
        for k in range(2):
            s = side * 2 + k
            hit = mine & (rank == float(k))
            found = jnp.sum(jnp.where(hit, local, 0.0), axis=1, keepdims=True).astype(jnp.int32) - 1
            for b in range(4):
                hot[b, s * 64:(s + 1) * 64, :] = (
                    (found[b * 64:(b + 1) * 64] == iota((64, ROWS), 1)).astype(F32).astype(BF)
                )

    def spread(s, n, part):
        for h in range(2):
            stage[h, pl.ds(s * 4 + n, 64, stride=16), :] = part[:, h * 128:(h + 1) * 128]

    def pack(dst, b):
        @pl.loop(0, 4)
        def _(i):
            rows = pl.ds(i * 256, 256)
            both = jnp.concatenate([stage[0, rows, :], stage[1, rows, :]], axis=1)
            dst[pl.ds(b * 64 + i * 16, 16)] = both.astype(BF).reshape(16, 16, 256)

    def unpack(src, b):
        @pl.loop(0, 4)
        def _(i):
            rows = pl.ds(i * 256, 256)
            both = src[pl.ds(b * 64 + i * 16, 16)].reshape(256, 256).astype(F32)
            stage[0, rows, :] = both[:, :128]
            stage[1, rows, :] = both[:, 128:]

    def collect(ss, n):
        out = []
        for s in ss:
            rows = pl.ds(s * 4 + n, 64, stride=16)
            out.append(jnp.concatenate([stage[0, rows, :], stage[1, rows, :]], axis=1))
        return jnp.concatenate(out, axis=0).astype(BF)

    def send_pair(src, dst, p, sem, first=0, last=8):
        @pl.loop(first, last)
        def _(k):
            cc = (c + k // 4) % 2
            for j in (p, p + 2):
                yy = (y + j) % 4
                xx = (x + (k + j - p) % 4) % 4

                def push(zz):
                    to = (yy * 4 + xx) * 16 + zz * 2 + cc
                    rcopy(src.at[to], dst.at[me], sem + j, ident(yy, zz, cc, xx)).start()

                if j == 0:
                    @pl.when(k > 0)
                    def _():
                        push(z)
                else:
                    push(z)
                for i in range(1, 8):
                    push((z + i) % 8)

    def wait_block(dst, j, sem):
        @pl.when(j == 0)
        def _():
            wait_recv(dst.at[pl.ds(0, 63)], sem)

        @pl.when(j > 0)
        def _():
            wait_recv(dst.at[pl.ds(0, 64)], sem + j)

    def wait_block_sent(src, sem):
        wait_send(src.at[pl.ds(0, 63)], sem)
        for j in range(1, 4):
            wait_send(src.at[pl.ds(0, 64)], sem + j)

    G, R = 2, 6
    loads[1].wait()

    for p in range(2):
        @pl.loop(0, 2)
        def _(i):
            b = (y + p + 2 * i) % 4
            for n in range(4):
                part = dot(hot[b], emb[:, n * 256:(n + 1) * 256])
                for s in range(4):
                    spread(s, n, part[s * 64:(s + 1) * 64])
            pack(send_g, b)

        send_pair(send_g, recv_g, p, G)

    recv_g[me] = send_g[me]

    earlier = iota((128, 128), 1) < iota((128, 128), 0)
    for side in range(2):
        row_owner = row_code[side] >> 9
        col_owner = col_code[side] >> 9
        rank = jnp.sum(jnp.where((col_owner == row_owner) & earlier, 1.0, 0.0), axis=1, keepdims=True)
        for b in range(4):
            home = col_owner == b * 64 + (lanes & 63)
            pick = jnp.where(home & (rank == (lanes >> 6).astype(F32)), 1.0, 0.0)
            picks[b, side] = pick.astype(BF)
            picks_t[b, side] = pick.T.astype(BF)
    feats[...] = jnp.zeros_like(feats)

    @pl.loop(0, 4)
    def _(b):
        hot_t[b] = hot[b].T

    loads[2].wait()
    loads[3].wait()

    @pl.loop(0, 8)
    def _(i):
        rows = pl.ds(pl.multiple_of(i * 256, 256), 256)
        for n in range(4):
            w1t[n * 256:(n + 1) * 256, rows] = w1[rows, n * 256:(n + 1) * 256].T

    @pl.loop(0, 4)
    def _(i):
        rows = pl.ds(pl.multiple_of(i * 256, 256), 256)
        for n in range(4):
            w2t[n * 256:(n + 1) * 256, rows] = w2[rows, n * 256:(n + 1) * 256].T

    @pl.loop(0, 4)
    def _(i):
        j = i % 2 * 2 + i // 2
        b = (y + 4 - j) % 4
        wait_block(recv_g, j, G)
        unpack(recv_g, b)
        for side in range(2):
            for n in range(4):
                cols = slice(side * 1024 + n * 256, side * 1024 + (n + 1) * 256)
                part = dot(picks[b, side], collect((side * 2, side * 2 + 1), n))
                feats[:, cols] = feats[:, cols] + part.astype(BF)

    other = ident(y, z, 1 - c, x)
    for n in range(4):
        cols = slice(n * 256, (n + 1) * 256)
        act, slope = gelu_both(dot(feats[...], w1[:, cols]))
        act = act.astype(BF)
        first_act[:, cols] = act
        first_slope[:, cols] = slope

    sgrad = jnp.sum(jnp.where(eye, sgrad_in[...], 0.0), axis=1, keepdims=True)
    for n in range(4):
        cols = slice(n * 256, (n + 1) * 256)
        act, slope = gelu_both(dot(first_act[...], w2[:, cols]))
        act = act.astype(BF)
        sw = sw_in[cols].reshape(1, 256)
        second_act[:, cols] = act
        d2[0:128, cols] = (sgrad * sw.astype(F32) * slope).astype(BF)
    rcopy(d2.at[pl.ds(0, 128)], d2.at[pl.ds(128, 128)], 12, other).start()

    for n in range(4):
        cols = slice(n * 256, (n + 1) * 256)
        back = dot(d2[0:128, :], w2t[:, cols])
        d1[0:128, cols] = (back * first_slope[:, cols]).astype(BF)
    rcopy(d1.at[pl.ds(0, 128)], d1.at[pl.ds(128, 128)], 14, other).start()

    for n in range(8):
        cols = slice(n * 256, (n + 1) * 256)
        fg[:, cols] = dot(d1[0:128, :], w1t[:, cols]).astype(BF)

    def return_pack(j):
        b = (y + j) % 4
        for side in range(2):
            for n in range(4):
                col = side * 1024 + n * 256
                part = dot(picks_t[b, side], fg[:, col:col + 256])
                for k in range(2):
                    spread(side * 2 + k, n, part[k * 64:(k + 1) * 64])
        pack(send_r, b)

    def return_pair(p):
        @pl.loop(0, 2)
        def _(i):
            return_pack(p + 2 * i)

    return_pair(0)
    send_pair(send_r, recv_r, 0, R, 0, 4)

    score = jnp.zeros((1, 128), F32)
    for n in range(4):
        cols = slice(n * 256, (n + 1) * 256)
        act = second_act[:, cols]
        hbuf[0, :, cols] = jnp.sum(sgrad * act.astype(F32), axis=0, keepdims=True)
        score += dot_nt(jnp.broadcast_to(sw_in[cols].reshape(1, 256), (8, 256)), act)[0:1]
    small_out[13:14, 0:128] = score
    rcopy(hbuf.at[0], hbuf.at[1], 13, other).start()

    for i in range(4):
        cols = slice(i * 256, (i + 1) * 256)
        at_own[i * 8:(i + 1) * 8] = first_act[:, cols].T.reshape(8, 2, 16, 128)
    rcopy(at_own.at[:, 1 - c], at.at[:, :, pl.ds(128, 128)], 11, other).start()
    at[:, :, 0:128] = at_own[:, c]
    for i in range(8):
        cols = slice(i * 256, (i + 1) * 256)
        ft_own[i * 4:(i + 1) * 4] = feats[:, cols].T.reshape(4, 2, 32, 128)
    rcopy(ft_own.at[:, 1 - c], ft.at[:, :, pl.ds(128, 128)], 10, other).start()
    ft[:, :, 0:128] = ft_own[:, c]

    wait_recv(at.at[:, :, pl.ds(0, 128)], 11)
    wait_recv(d2.at[pl.ds(0, 128)], 12)
    low = iota((8, 8, 512), 1) < 4

    @pl.loop(0, 4)
    def _(yy):
        res = dot(at[pl.ds(yy * 8, 8)].reshape(128, 256), d2[...]).reshape(8, 16, 1024)
        for pair in range(2):
            lo = res[:, pair * 8:(pair + 1) * 8, :512]
            hi = res[:, pair * 8:(pair + 1) * 8, 512:]
            even = jnp.where(low, lo, pltpu.roll(hi, 4, axis=1))
            odd = jnp.where(low, pltpu.roll(lo, 4, axis=1), hi)
            for bit, part in ((0, even), (1, odd)):
                full = jnp.concatenate([part[:, :, :256], part[:, :, 256:]], axis=1)
                pb[yy, pair * 2 + bit, :, :, 128:384] = full.astype(BF)

    wait_recv(ft.at[:, :, pl.ds(0, 128)], 10)
    wait_recv(d1.at[pl.ds(0, 128)], 14)

    @pl.loop(0, 4)
    def _(yy):
        lhs = ft[pl.ds(yy * 8, 8)].reshape(256, 256)
        for n in range(2):
            lo = dot(lhs, d1[:, n * 256:(n + 1) * 256]).reshape(8, 4, 8, 256)
            hi = dot(lhs, d1[:, 512 + n * 256:512 + (n + 1) * 256]).reshape(8, 4, 8, 256)
            for xx in range(4):
                full = jnp.concatenate([lo[:, xx], hi[:, xx]], axis=1).astype(BF)
                if n == 0:
                    pa[xx, yy, :, :, 0:256] = full
                else:
                    pa[xx, yy, :, :, 256:384] = full[:, :, :128]
                    pb[yy, xx, :, :, 0:128] = full[:, :, 128:]

    def along(axis, k):
        if axis == "x":
            return ident(y, z, c, (x + k) % 4), (x + k) % 4
        if axis == "y":
            return ident((y + k) % 4, z, c, x), (y + k) % 4
        return ident(y, (z + k) % 8, c, x), (z + k) % 8

    for k in range(1, 4):
        dev, at_x = along("x", k)
        rcopy(pa.at[at_x], ra.at[k - 1], 15, dev).start()
        dev, at_y = along("y", k)
        rcopy(pb.at[at_y], rb.at[k - 1], 16, dev).start()

    def head_step(base, count, axis, mine, sem):
        for k in range(1, count):
            dev, _ = along(axis, k)
            rcopy(hbuf.at[base + mine], hbuf.at[base + mine], sem, dev).start()

    wait_recv(hbuf.at[0], 13)
    wait_send(hbuf.at[0], 13)
    hbuf[2 + x] = hbuf[0] + hbuf[1]
    head_step(2, 4, "x", x, 17)

    send_pair(send_r, recv_r, 0, R, 4, 8)
    return_pair(1)


    wait_recv(hbuf.at[pl.ds(2, 3)], 17)
    wait_send(hbuf.at[pl.ds(2, 3)], 17)
    hbuf[6 + y] = hbuf[2] + hbuf[3] + hbuf[4] + hbuf[5]
    head_step(6, 4, "y", y, 20)

    send_pair(send_r, recv_r, 1, R, 0, 4)

    node[...] = jnp.zeros_like(node)

    def land_block(j):
        b = (y + 4 - j) % 4
        wait_block(recv_r, j, R)
        unpack(recv_r, b)
        for n in range(4):
            cols = slice(n * 256, (n + 1) * 256)
            node[:, cols] = node[:, cols] + dot(hot_t[b], collect((0, 1, 2, 3), n))

    def add4(own, got, out, sec):
        total = own[sec].astype(F32) + got[0, sec].astype(F32) + got[1, sec].astype(F32) + got[2, sec].astype(F32)
        out[sec] = total.astype(BF)

    wait_recv(ra, 15)

    @pl.loop(0, 4)
    def _(i):
        add4(pa.at[x], ra, sa, i)

    for k in range(1, 4):
        dev, at_y = along("y", k)
        rcopy(sa.at[at_y], r2a.at[k - 1], 18, dev).start()
    wait_recv(rb, 16)

    @pl.loop(0, 4)
    def _(i):
        add4(pb.at[y], rb, sb, i)

    for k in range(1, 4):
        dev, at_x = along("x", k)
        rcopy(sb.at[at_x], r2b.at[k - 1], 19, dev).start()

    send_pair(send_r, recv_r, 1, R, 4, 8)
    recv_r[me] = send_r[me]

    wait_recv(hbuf.at[pl.ds(6, 3)], 20)
    wait_send(hbuf.at[pl.ds(6, 3)], 20)
    hbuf[10 + z] = hbuf[6] + hbuf[7] + hbuf[8] + hbuf[9]
    head_step(10, 8, "z", z, 23)

    @pl.loop(0, 1)
    def _(j):
        land_block(j)

    wait_recv(r2a, 18)
    total = sa[y].astype(F32) + r2a[0].astype(F32) + r2a[1].astype(F32) + r2a[2].astype(F32)
    ta[...] = total.astype(BF)
    for k in range(1, 8):
        dev, at_z = along("z", k)
        rcopy(ta.at[at_z], r3a.at[k - 1], 21, dev).start()
    wait_recv(r2b, 19)
    total = sb[x].astype(F32) + r2b[0].astype(F32) + r2b[1].astype(F32) + r2b[2].astype(F32)
    tb[...] = total.astype(BF)
    for k in range(1, 8):
        dev, at_z = along("z", k)
        rcopy(tb.at[at_z], r3b.at[k - 1], 22, dev).start()

    @pl.loop(2, 3)
    def _(j):
        land_block(j)

    wait_recv(r3a, 21)
    wait_recv(r3b, 22)
    left = ta[z].astype(F32)
    right = tb[z].astype(F32)
    for k in range(7):
        left += r3a[k].astype(F32)
        right += r3b[k].astype(F32)
    whole = jnp.concatenate([left, right], axis=1)
    small_out[0:8, 0:512] = whole[0:8, 0:512]
    small_out[0:8, 512:1024] = whole[8:16, 0:512]
    small_out[8:12, 0:256] = whole[0:4, 512:768]
    small_out[8:12, 512:768] = whole[4:8, 512:768]
    small_out[8:12, 256:512] = whole[8:12, 512:768]
    small_out[8:12, 768:1024] = whole[12:16, 512:768]

    wait_recv(hbuf.at[pl.ds(10, 7)], 23)
    head = hbuf[10]
    for k in range(1, 8):
        head += hbuf[10 + k]
    small_out[12:13, :] = head

    land_block(1)
    b = (y + 1) % 4
    wait_block(recv_r, 3, R)
    unpack(recv_r, b)
    outs = []
    for n in range(4):
        cols = slice(n * 256, (n + 1) * 256)
        node[:, cols] = node[:, cols] + dot(hot_t[b], collect((0, 1, 2, 3), n))
        outs.append(pltpu.make_async_copy(node.at[:, cols], node_out.at[:, cols], load_sem.at[n]))
        outs[n].start()

    wait_send(fifteen, 0)
    wait_send(idx.at[pl.ds(0, 240)], 1)
    wait_block_sent(send_g, G)
    wait_block_sent(send_r, R)
    wait_send(ft.at[:, :, pl.ds(0, 128)], 10)
    wait_send(at.at[:, :, pl.ds(0, 128)], 11)
    wait_send(d2.at[pl.ds(0, 128)], 12)
    wait_send(d1.at[pl.ds(0, 128)], 14)
    wait_send(ra, 15)
    wait_send(rb, 16)
    wait_send(r2a, 18)
    wait_send(r2b, 19)
    wait_send(r3a, 21)
    wait_send(r3b, 22)
    wait_send(hbuf.at[pl.ds(10, 7)], 23)
    for out in outs:
        out.wait()


def deliver(node_in, small_in, score_out, node_out, first_out, second_out, head_out, held, small, sem_in, sem_out):
    spans = [pl.ds(i * 96, 96) for i in range(4)]
    ins = [pltpu.make_async_copy(node_in.at[p], held.at[p], sem_in.at[i]) for i, p in enumerate(spans)]
    outs = [pltpu.make_async_copy(held.at[p], node_out.at[p], sem_out.at[i]) for i, p in enumerate(spans)]
    rest = pltpu.make_async_copy(small_in, small, sem_in.at[4])
    for copy in ins + [rest]:
        copy.start()
    for i in range(4):
        ins[i].wait()
        outs[i].start()
    rest.wait()
    score_out[...] = small[13:14, 0:128].reshape(128)
    first_out[...] = small[0:8, :]
    second_out[...] = small[8:12, :]
    head_out[...] = small[12:13, :].reshape(HID)
    for copy in outs:
        copy.wait()


def shards(
    embeddings, endpoint_pairs, node_slot, first_weight, second_weight, score_weight, score_grad
):
    vm = pl.BlockSpec(memory_space=pltpu.VMEM)
    hbm = pl.BlockSpec(memory_space=pltpu.HBM)
    V = pltpu.VMEM
    scratch = [
        V((NODES // 128, 128), jnp.int32), V((ROWS, WIDTH), BF), V((2 * WIDTH, HID), BF), V((HID, HID), BF),
        V((HID, 2 * WIDTH), BF), V((HID, HID), BF),
        V((NDEV, 2 * EDGES), jnp.int32), V((4, NDEV, ROWS), BF), V((4, ROWS, NDEV), BF),
        V((4, 2, EDGES, 128), BF), V((4, 2, 128, EDGES), BF), V((2, 64 * 16, 128), F32),
        V((NDEV, 16, 256), BF), V((NDEV, 16, 256), BF), V((NDEV, 16, 256), BF), V((NDEV, 16, 256), BF),
        V((EDGES, 2 * WIDTH), BF), V((EDGES, HID), BF), V((EDGES, HID), F32),
        V((32, 2, 32, EDGES), BF), V((32, 32, 2 * EDGES), BF),
        V((32, 2, 16, EDGES), BF), V((32, 16, 2 * EDGES), BF),
        V((2 * EDGES, HID), BF), V((2 * EDGES, HID), BF), V((EDGES, 2 * WIDTH), BF),
        V((4, 4, 8, 16, 384), BF), V((4, 4, 8, 16, 384), BF),
        V((3, 4, 8, 16, 384), BF), V((3, 4, 8, 16, 384), BF),
        V((4, 8, 16, 384), BF), V((4, 8, 16, 384), BF),
        V((3, 8, 16, 384), BF), V((3, 8, 16, 384), BF),
        V((8, 16, 384), BF), V((8, 16, 384), BF),
        V((7, 16, 384), BF), V((7, 16, 384), BF),
        V((18, 1, HID), F32), V((ROWS, WIDTH), F32), V((EDGES, HID), BF),
        V((15, 1, 2 * EDGES), jnp.int32),
        pltpu.SemaphoreType.DMA((4,)), pltpu.SemaphoreType.DMA((24,)), pltpu.SemaphoreType.DMA((24,)),
    ]
    node, small = pl.pallas_call(
        body,
        out_shape=(
            jax.ShapeDtypeStruct((ROWS, WIDTH), F32),
            jax.ShapeDtypeStruct((16, HID), F32),
        ),
        in_specs=[vm] * 3 + [hbm] * 4,
        out_specs=(hbm, vm),
        scratch_shapes=scratch,
        compiler_params=pltpu.CompilerParams(
            collective_id=0, has_side_effects=True, vmem_limit_bytes=58 * 2**20
        ),
    )(
        endpoint_pairs.T, score_grad.reshape(1, EDGES), score_weight,
        node_slot.reshape(NODES // 128, 128), embeddings, first_weight, second_weight,
    )
    return pl.pallas_call(
        deliver,
        out_shape=(
            jax.ShapeDtypeStruct((EDGES,), F32),
            jax.ShapeDtypeStruct((ROWS, WIDTH), F32),
            jax.ShapeDtypeStruct((8, HID), F32),
            jax.ShapeDtypeStruct((4, HID), F32),
            jax.ShapeDtypeStruct((HID,), F32),
        ),
        in_specs=[hbm, hbm],
        out_specs=(vm, hbm, vm, vm, vm),
        scratch_shapes=[
            V((ROWS, WIDTH), F32), V((16, HID), F32), pltpu.SemaphoreType.DMA((5,)), pltpu.SemaphoreType.DMA((4,)),
        ],
    )(node, small)


def solution(mesh):
    both = P(("dom", "rep"))
    rows = P(("dom", "rep"), None)
    return jax.shard_map(
        shards,
        mesh=mesh,
        in_specs=(rows, rows, P(), P(), P(), P(), both),
        out_specs=(both, rows, rows, rows, P()),
        check_vma=False,
    )
```
